32 devices in a mesh: groups: 2 (over y), block: 16 (over z, x, core).
Axes of the slice: x: 2, y: 2, z: 4, core: 2. Of those that a mesh axis runs over, the one named last changes fastest.
Arguments:
- tokens: bfloat16 [4096, 2048], P(('groups', 'block')), parts along dimension 0, may hold values from -6 to 6
- expert_ids: int32 [4096, 8], P(('groups', 'block')), parts along dimension 0, may hold values from 0 to 15, all different within a row; in each aligned block of 128 rows (0 to 127, 128 to 255, ...) at most 96 rows name the same one
- route_weight: float32 [4096, 8], P(('groups', 'block')), parts along dimension 0, may hold values from 0.1 to 1
- memory_keep: float32 [32, 2048], P(('groups', 'block')), parts along dimension 0, may hold values from 0 to 1
- mem_keys: bfloat16 [32, 2048], replicated, may hold values from -4 to 4
- w_gate: bfloat16 [16, 2048, 768], P('block'), may hold values from -0.125 to 0.125
- w_up: bfloat16 [16, 2048, 768], P('block'), may hold values from -0.125 to 0.125
- w_down: bfloat16 [16, 768, 2048], P('block'), may hold values from -0.21875 to 0.21875
Outputs:
- mixed: bfloat16 [4096, 2048], P(('groups', 'block')), parts along dimension 0
- memory_state: float32 [1024, 2048], P(('groups', 'block')), parts along dimension 0
The draws below stay inside these ranges and needn't reach their ends.
There are 2 independent parts, one for each index of `groups`. The reference program is written for one: setup_inputs(seed, part) draws one part's arguments, and reference() takes and returns one part's arrays. A program takes and returns all parts, laid end to end along the dimension named above; an argument that names none is the same for every part. Nothing has to cross between parts.
Inputs may be any that keep to these rules, and one draw needn't show every extreme that they name: `expert_ids`: in each aligned block of 128 rows (the rows of one clip) no expert is named by more than 96 rows; a row names 8 different experts.
All inputs are finite; a program needn't handle non-finite values.
Results may differ from the reference program's by a relative error of at most 0.0058.
Values may be sent and summed in bfloat16 or wider, within the bound.
A program may use at most 192 MiB of HBM per device.

```python
import math
import jax
import jax.numpy as jnp
import numpy as np
from jax import lax

D = 2048
FF = 768
TOPK = 8
CLIP_VIDEO_TOKENS = 128
MEM = 32
SPECIALIST_TOTAL = 16
SEGMENT_TOTAL = 16
CAP = 96
TOKENS = 2048


def draw_tokens(key, part):
    key = jax.random.fold_in(key, 5)
    entry_key = jax.random.fold_in(key, 0)
    drawn = jax.random.truncated_normal(entry_key, -6.0, 6.0, (TOKENS, D), jnp.float32)
    values = drawn
    return values.astype(jnp.bfloat16)


def draw_memory_keep(key, part):
    key = jax.random.fold_in(key, 11)
    stochastic_seeds = jax.random.split(key, 6)
    share = 0.5
    slow = jax.random.bernoulli(stochastic_seeds[0], share, (1, D))
    factor = jnp.exp(jax.random.uniform(stochastic_seeds[1], (SEGMENT_TOTAL, D), jnp.float32, -0.6931, 0.6931))
    slow_rate = jax.random.uniform(stochastic_seeds[2], (1, D), jnp.float32, 0.05, 0.4) * 2.3026 / SEGMENT_TOTAL
    fast_rate = jax.random.uniform(stochastic_seeds[3], (1, D), jnp.float32, 0.1, 0.5)
    persistence_probability = jnp.where(slow, slow_rate, fast_rate) * factor
    spell_duration = jax.random.bernoulli(stochastic_seeds[4], 3.0 / SEGMENT_TOTAL, (SEGMENT_TOTAL, 1))
    threshold_position = jax.random.uniform(stochastic_seeds[5], (SEGMENT_TOTAL, 1), jnp.float32, 0.5, 0.8)
    survival_flags = jnp.exp(-persistence_probability) * jnp.where(spell_duration, threshold_position, 1.0)
    return survival_flags.astype(jnp.float32)


def block_scale(rng, extent, cuts, smallest, largest):
    def one(dim, shards_of):
        steps = jax.random.uniform(jax.random.fold_in(jax.random.fold_in(rng, 6), dim), (shards_of,), jnp.float32, smallest / len(cuts), largest / len(cuts))
        return jnp.repeat(jnp.exp(steps), extent[dim] // shards_of).reshape((-1,) + (1,) * (len(extent) - dim - 1))

    loudness = one(*cuts[0])
    for cut in cuts[1:]:
        loudness = loudness * one(*cut)
    return loudness


def routed_block(key, own, number, rows, count, top, reach, slope):
    sequence = jax.random.permutation(key, count)
    crowded, common = load_shares(count, rows * top, reach, slope, True), load_shares(count, rows * top, reach, slope, False)
    places = jnp.arange(count)

    def named(tallies, turn):
        used = int((tallies > 0).sum())
        fixed = max(1, used // 4)
        shifted = fixed + (places - fixed + turn * (used - fixed)) % max(1, count - fixed)
        return jnp.zeros((count,), jnp.int32).at[sequence[jnp.where(places < fixed, places, shifted)]].set(jnp.asarray(tallies, jnp.int32))

    tallies = jnp.where(number % 4 == 0, named(crowded, number // 4), named(common, number - number // 4 - 1))
    mixed = jax.random.permutation(jax.random.fold_in(own, 3), count)
    giver, taker = mixed[0:count // 2 * 2:2], mixed[1:count // 2 * 2:2]
    slack = jnp.minimum(tallies[giver] - 1, reach - tallies[taker]) // 2
    slack = jnp.where((giver == sequence[0]) | (taker == sequence[0]) | (tallies[taker] == 0), 0, jnp.maximum(slack, 0))
    shifted = jax.random.randint(jax.random.fold_in(own, 4), (count // 2,), 0, 1 << 20) % (slack + 1)
    tallies = tallies.at[giver].add(-shifted).at[taker].add(shifted)
    labels = jnp.searchsorted(jnp.cumsum(tallies), jnp.arange(rows * top), side="right").astype(jnp.int32)
    grid = labels.reshape(top, rows).T
    grid = grid[jax.random.permutation(jax.random.fold_in(own, 1), rows)]
    turn = jax.random.randint(jax.random.fold_in(own, 2), (rows, 1), 0, top)
    return jnp.take_along_axis(grid, (jnp.arange(top)[None, :] + turn) % top, axis=1)


def load_shares(amount, total, bound, skew, full):
    weights = [(1 << 20) // math.isqrt(standing ** skew) + 1 for standing in range(1, amount + 1)]
    largest = bound if full else min(bound, max(-(-total // amount), total * weights[0] // sum(weights)))
    least = 1 if total - largest >= amount - 1 else 0
    given, spare = [largest] + [least] * (amount - 1), total - largest - least * (amount - 1)
    while spare > 0:
        movable = [i for i in range(1, amount) if given[i] < largest] or [i for i in range(1, amount) if given[i] < bound]
        mass, left = sum([weights[i] for i in movable]), spare
        for i in movable:
            addition = min(bound - given[i], max(1, left * weights[i] // mass), spare)
            given[i] = given[i] + addition
            spare = spare - addition
    return np.array(given)


def normal_values(stream_key, dims, deviation, most, cuts=(), held_as=jnp.bfloat16):
    factor_of = block_scale(stream_key, dims, cuts, -0.22, 0.18) if cuts else 1.0
    entries = jax.random.normal(stream_key, dims, jnp.float32) * deviation * factor_of
    return jnp.minimum(jnp.maximum(entries, -most), most).astype(held_as)


def setup_inputs(seed: int = 0, part: int = 0) -> dict:
    arg_keys = jax.random.split(jax.random.key(seed), 9)
    part_keys = jax.random.split(jax.random.fold_in(arg_keys[8], part), 9)
    tokens = draw_tokens(jax.random.fold_in(jax.random.fold_in(arg_keys[8], part), 71), part)
    expert_ids_keys = jax.random.split(jax.random.fold_in(part_keys[1], 1), TOKENS // CLIP_VIDEO_TOKENS)
    expert_ids_turns = jax.random.permutation(jax.random.fold_in(part_keys[1], 3), TOKENS // CLIP_VIDEO_TOKENS)
    expert_ids = jax.vmap(lambda own, number: routed_block(jax.random.fold_in(part_keys[1], 2), own, number, CLIP_VIDEO_TOKENS, SPECIALIST_TOTAL, TOPK, CAP, 2))(expert_ids_keys, expert_ids_turns).reshape((TOKENS, TOPK))
    route_weight = jnp.clip(jnp.exp(math.log(1.0) - 2.3025851 * jax.random.uniform(part_keys[2], (TOKENS, TOPK), jnp.float32) ** block_scale(part_keys[2], (TOKENS, TOPK), ((0, 16),), -0.2, 0.2)), 0.1, 1.0)
    memory_keep = draw_memory_keep(jax.random.fold_in(jax.random.fold_in(arg_keys[8], part), 71), part)
    mem_keys = normal_values(arg_keys[4], (MEM, D), 1.0, 4.0)
    w_gate = normal_values(arg_keys[5], (SPECIALIST_TOTAL, D, FF), D ** -0.5, 0.125, ((0, 16),))
    w_up = normal_values(arg_keys[6], (SPECIALIST_TOTAL, D, FF), D ** -0.5, 0.125, ((0, 16),))
    w_down = normal_values(arg_keys[7], (SPECIALIST_TOTAL, FF, D), FF ** -0.5, 0.21875, ((0, 16),))
    return {"tokens": tokens, "expert_ids": expert_ids, "route_weight": route_weight, "memory_keep": memory_keep, "mem_keys": mem_keys, "w_gate": w_gate, "w_up": w_up, "w_down": w_down}


def slots_of(row):
    hot = (row[:, None] == jnp.arange(SPECIALIST_TOTAL, dtype=jnp.int32)[None, :]).astype(jnp.int32)
    return jnp.sum((jnp.cumsum(hot, axis=0) - hot) * hot, axis=1).astype(jnp.int32)


def one_expert(operands):
    rows, gate_w, up_w, down_w = operands
    gate = jnp.dot(rows, gate_w, preferred_element_type=jnp.float32)
    upper = jnp.dot(rows, up_w, preferred_element_type=jnp.float32)
    hidden = (jax.nn.silu(gate) * upper).astype(jnp.bfloat16)
    return jnp.dot(hidden, down_w, preferred_element_type=jnp.float32).astype(jnp.bfloat16)


def reference(tokens, expert_ids, route_weight, memory_keep, mem_keys, w_gate, w_up, w_down):
    ids = expert_ids.reshape(SEGMENT_TOTAL, CLIP_VIDEO_TOKENS * TOPK)
    slot = lax.map(slots_of, ids)
    anchor = jnp.arange(SEGMENT_TOTAL, dtype=jnp.int32)[:, None]
    dest = ((ids * SEGMENT_TOTAL + anchor) * CAP + slot).astype(jnp.int32).reshape(-1)
    rows = jnp.repeat(tokens, TOPK, axis=0)
    buffer = jnp.zeros((SPECIALIST_TOTAL * SEGMENT_TOTAL * CAP, D), jnp.bfloat16).at[dest].set(rows)
    buffer = buffer.reshape(SPECIALIST_TOTAL, SEGMENT_TOTAL * CAP, D)
    outputs = lax.map(one_expert, (buffer, w_gate, w_up, w_down)).reshape(SPECIALIST_TOTAL * SEGMENT_TOTAL * CAP, D)
    partner_target = dest.reshape(TOKENS, TOPK)
    moe = jnp.zeros((TOKENS, D), jnp.float32)
    for choice_k in range(TOPK):
        moe = moe + outputs[partner_target[:, choice_k]].astype(jnp.float32) * route_weight[:, choice_k:choice_k + 1]
    scale_d = D ** -0.5
    scale_m = MEM ** -0.5
    clips_x = tokens.reshape(SEGMENT_TOTAL, CLIP_VIDEO_TOKENS, D)

    def clip_step(state, inputs):
        block_x, survival_flags = inputs
        scores = (jnp.dot(block_x, mem_keys.T, preferred_element_type=jnp.float32) * scale_d).astype(jnp.bfloat16)
        write = jnp.dot(scores.T, block_x, preferred_element_type=jnp.float32) / CLIP_VIDEO_TOKENS
        memory_read = state.astype(jnp.bfloat16)
        read_scores = (jnp.dot(block_x, memory_read.T, preferred_element_type=jnp.float32) * scale_d).astype(jnp.bfloat16)
        recall = jnp.dot(read_scores, memory_read, preferred_element_type=jnp.float32) * scale_m
        new_state = survival_flags[None, :] * state + write
        return new_state, (recall, new_state)

    start = jnp.zeros((MEM, D), jnp.float32)
    _, (recalls, states) = lax.scan(clip_step, start, (clips_x, memory_keep))
    mixed = (moe + recalls.reshape(TOKENS, D)).astype(jnp.bfloat16)
    return mixed, states.reshape(SEGMENT_TOTAL * MEM, D)
```

```python
import jax
import jax.numpy as jnp
from jax import lax
from jax.sharding import PartitionSpec as P


def prefix(value, axis, join, neutral):
    count, mine = (lax.axis_size(axis), lax.axis_index(axis))
    pieces = jax.tree.map(lambda part: lax.all_gather(part, axis), value)
    subtotal = jax.tree.map(
        lambda part, zero: jnp.full_like(part, 0) + jnp.asarray(zero, part.dtype), value, neutral
    )

    def lap(position, subtotal):
        longer = join(subtotal, jax.tree.map(lambda part: part[position], pieces))
        return jax.tree.map(lambda new, old: jnp.where(position < mine, new, old), longer, subtotal)

    return lax.fori_loop(0, count - 1, lap, subtotal)


def run_expert(received, gate_w, up_w, down_w):
    count, slots, width = received.shape
    flat = received.reshape(count * slots, width)
    gate = jnp.dot(flat, gate_w, preferred_element_type=jnp.float32)
    upper = jnp.dot(flat, up_w, preferred_element_type=jnp.float32)
    hidden = (jax.nn.silu(gate) * upper).astype(jnp.bfloat16)
    produced = jnp.dot(hidden, down_w, preferred_element_type=jnp.float32).astype(jnp.bfloat16)
    return produced.reshape(count, slots, width)


def chain(earlier, later):
    return (earlier[0] * later[0], later[0][None, :] * earlier[1] + later[1])


def sparse_moe(tokens, expert_ids, route_weight, w_gate, w_up, w_down):
    tok_rows, width = tokens.shape
    topk = expert_ids.shape[1]
    experts = lax.axis_size("block")
    capacity = max(2, (3 * tok_rows * topk + 2 * experts - 1) // (2 * experts))
    pairs = expert_ids.reshape(-1)
    onehot = (pairs[:, None] == jnp.arange(experts, dtype=jnp.int32)[None, :]).astype(jnp.int32)
    slot = jnp.sum((jnp.cumsum(onehot, axis=0) - onehot) * onehot, axis=1)
    dest = pairs * capacity + slot
    source_rows = jnp.repeat(tokens, topk, axis=0)
    outgoing = jnp.zeros((experts * capacity, width), jnp.bfloat16).at[dest].set(source_rows)
    outgoing = outgoing.reshape(experts, capacity, width)
    received = lax.all_to_all(outgoing, "block", split_axis=0, concat_axis=0, tiled=True)
    produced = run_expert(received, w_gate[0], w_up[0], w_down[0])
    returned = lax.all_to_all(produced, "block", split_axis=0, concat_axis=0, tiled=True)
    picked = returned.reshape(experts * capacity, width)[dest]
    weighted = picked.astype(jnp.float32).reshape(tok_rows, topk, width) * route_weight[:, :, None]
    return jnp.sum(weighted, axis=1)


def sparse(tokens, expert_ids, route_weight, memory_keep, mem_keys, w_gate, w_up, w_down):
    tok_rows, width = tokens.shape
    moe = sparse_moe(tokens, expert_ids, route_weight, w_gate, w_up, w_down)
    scale_d = width ** (-0.5)
    scores = (jnp.dot(tokens, mem_keys.T, preferred_element_type=jnp.float32) * scale_d).astype(
        jnp.bfloat16
    )
    write = jnp.dot(scores.T, tokens, preferred_element_type=jnp.float32) / tok_rows
    survival_flags = memory_keep[0]
    identity = (jnp.ones_like(survival_flags), jnp.zeros_like(write))
    _, memory_in = prefix((survival_flags, write), "block", chain, identity)
    memory_state = survival_flags[None, :] * memory_in + write
    return finish(tokens, moe, memory_in), memory_state


def finish(tokens, moe, memory_in):
    scale_d = tokens.shape[1] ** (-0.5)
    scale_m = memory_in.shape[0] ** (-0.5)
    memory_read = memory_in.astype(jnp.bfloat16)
    read_scores = (
        jnp.dot(tokens, memory_read.T, preferred_element_type=jnp.float32) * scale_d
    ).astype(jnp.bfloat16)
    recall = jnp.dot(read_scores, memory_read, preferred_element_type=jnp.float32) * scale_m
    return (moe.astype(jnp.float32) + recall).astype(jnp.bfloat16)


def dense(tokens, expert_ids, route_weight, memory_keep, mem_keys, w_gate, w_up, w_down):
    rows, width = tokens.shape
    count, mine = lax.axis_size("block"), lax.axis_index("block")
    hot = expert_ids[:, :, None] == jnp.arange(count, dtype=jnp.int32)[None, None, :]
    shares = jnp.sum(jnp.where(hot, route_weight[:, :, None], 0.0), axis=1)
    shares = lax.all_gather(shares, "block", axis=0, tiled=True)
    keeps = lax.all_gather(memory_keep, "block", axis=0, tiled=True)
    everyone = lax.all_gather(tokens, "block", axis=0, tiled=True)
    share = lax.dynamic_slice_in_dim(shares, mine, 1, axis=1)
    gate = jnp.dot(everyone, w_gate[0], preferred_element_type=jnp.float32)
    upper = jnp.dot(everyone, w_up[0], preferred_element_type=jnp.float32)
    hidden = (jax.nn.silu(gate) * upper).astype(jnp.bfloat16)
    produced = jnp.dot(hidden, w_down[0], preferred_element_type=jnp.float32)
    produced = (produced * share).astype(jnp.bfloat16)
    moe = lax.psum_scatter(produced, "block", scatter_dimension=0, tiled=True)

    scale_d = width ** (-0.5)
    scores = (jnp.dot(everyone, mem_keys.T, preferred_element_type=jnp.float32) * scale_d).astype(
        jnp.bfloat16
    )
    clips = everyone.reshape(count, rows, width)
    writes = (
        jnp.einsum(
            "ctm,ctd->cmd",
            scores.reshape(count, rows, -1),
            clips,
            preferred_element_type=jnp.float32,
        )
        / rows
    )
    memory_in = jnp.zeros(writes.shape[1:], jnp.float32)
    for clip in range(count - 1):
        longer = keeps[clip][None, :] * memory_in + writes[clip]
        memory_in = jnp.where(clip < mine, longer, memory_in)
    own = lax.dynamic_index_in_dim(writes, mine, axis=0, keepdims=False)
    memory_state = memory_keep * memory_in + own
    return finish(tokens, moe, memory_in), memory_state


def solution(mesh):
    experts = mesh.shape["block"]

    def shards(tokens, expert_ids, *rest):
        few = experts <= 4 * expert_ids.shape[1]
        return (dense if few else sparse)(tokens, expert_ids, *rest)

    return jax.shard_map(
        shards,
        mesh=mesh,
        in_specs=(
            P(("groups", "block"), None),
            P(("groups", "block"), None),
            P(("groups", "block"), None),
            P(("groups", "block"), None),
            P(),
            P("block", None, None),
            P("block", None, None),
            P("block", None, None),
        ),
        out_specs=(P(("groups", "block"), None), P(("groups", "block"), None)),
        check_vma=False,
    )
```

```python
import functools

import jax
import jax.numpy as jnp
from jax import lax
from jax.experimental import pallas as pl
from jax.experimental.pallas import tpu as pltpu
from jax.sharding import PartitionSpec as P


def prefix(value, axis, join, neutral):
    count, mine = (lax.axis_size(axis), lax.axis_index(axis))
    pieces = jax.tree.map(lambda part: lax.all_gather(part, axis), value)
    subtotal = jax.tree.map(
        lambda part, zero: jnp.full_like(part, 0) + jnp.asarray(zero, part.dtype), value, neutral
    )

    def lap(position, subtotal):
        longer = join(subtotal, jax.tree.map(lambda part: part[position], pieces))
        return jax.tree.map(lambda new, old: jnp.where(position < mine, new, old), longer, subtotal)

    return lax.fori_loop(0, count - 1, lap, subtotal)


def run_expert(received, gate_w, up_w, down_w):
    count, slots, width = received.shape
    flat = received.reshape(count * slots, width)
    gate = jnp.dot(flat, gate_w, preferred_element_type=jnp.float32)
    upper = jnp.dot(flat, up_w, preferred_element_type=jnp.float32)
    hidden = (jax.nn.silu(gate) * upper).astype(jnp.bfloat16)
    produced = jnp.dot(hidden, down_w, preferred_element_type=jnp.float32).astype(jnp.bfloat16)
    return produced.reshape(count, slots, width)


def chain(earlier, later):
    return (earlier[0] * later[0], later[0][None, :] * earlier[1] + later[1])


def sparse_moe(tokens, expert_ids, route_weight, w_gate, w_up, w_down):
    tok_rows, width = tokens.shape
    topk = expert_ids.shape[1]
    experts = lax.axis_size("block")
    capacity = max(2, (3 * tok_rows * topk + 2 * experts - 1) // (2 * experts))
    pairs = expert_ids.reshape(-1)
    onehot = (pairs[:, None] == jnp.arange(experts, dtype=jnp.int32)[None, :]).astype(jnp.int32)
    slot = jnp.sum((jnp.cumsum(onehot, axis=0) - onehot) * onehot, axis=1)
    dest = pairs * capacity + slot
    source_rows = jnp.repeat(tokens, topk, axis=0)
    outgoing = jnp.zeros((experts * capacity, width), jnp.bfloat16).at[dest].set(source_rows)
    outgoing = outgoing.reshape(experts, capacity, width)
    received = lax.all_to_all(outgoing, "block", split_axis=0, concat_axis=0, tiled=True)
    produced = run_expert(received, w_gate[0], w_up[0], w_down[0])
    returned = lax.all_to_all(produced, "block", split_axis=0, concat_axis=0, tiled=True)
    picked = returned.reshape(experts * capacity, width)[dest]
    weighted = picked.astype(jnp.float32).reshape(tok_rows, topk, width) * route_weight[:, :, None]
    return jnp.sum(weighted, axis=1)


def sparse(tokens, expert_ids, route_weight, memory_keep, mem_keys, w_gate, w_up, w_down):
    tok_rows, width = tokens.shape
    moe = sparse_moe(tokens, expert_ids, route_weight, w_gate, w_up, w_down)
    scale_d = width ** (-0.5)
    scores = (jnp.dot(tokens, mem_keys.T, preferred_element_type=jnp.float32) * scale_d).astype(
        jnp.bfloat16
    )
    write = jnp.dot(scores.T, tokens, preferred_element_type=jnp.float32) / tok_rows
    survival_flags = memory_keep[0]
    identity = (jnp.ones_like(survival_flags), jnp.zeros_like(write))
    _, memory_in = prefix((survival_flags, write), "block", chain, identity)
    memory_state = survival_flags[None, :] * memory_in + write
    return finish(tokens, moe, memory_in), memory_state


def finish(tokens, moe, memory_in):
    scale_d = tokens.shape[1] ** (-0.5)
    scale_m = memory_in.shape[0] ** (-0.5)
    memory_read = memory_in.astype(jnp.bfloat16)
    read_scores = (
        jnp.dot(tokens, memory_read.T, preferred_element_type=jnp.float32) * scale_d
    ).astype(jnp.bfloat16)
    recall = jnp.dot(read_scores, memory_read, preferred_element_type=jnp.float32) * scale_m
    return (moe.astype(jnp.float32) + recall).astype(jnp.bfloat16)


def dot(a, b, ca=1, cb=0):
    return lax.dot_general(a, b, (((ca,), (cb,)), ((), ())), preferred_element_type=jnp.float32)


def dense_kernel(
    count,
    tokens_ref,
    aux_ref,
    keys_ref,
    gate_ref,
    up_ref,
    down_ref,
    mixed_ref,
    state_ref,
    clips,
    aux,
    gate_w,
    up_w,
    down_w,
    kept,
    given,
    taken,
    landed,
    writes,
    base,
    load_sem,
    ring_send,
    ring_recv,
    twin_send,
    twin_recv,
    given_send,
    taken_recv,
    sum_send,
    sum_recv,
):
    turn = count // 2
    line = turn // 2
    half = turn // 2
    rows, width = tokens_ref.shape
    hidden_width = gate_w.shape[1]
    mem = keys_ref.shape[0]
    me = lax.axis_index("block")
    core = lax.rem(me, 2)
    my_x = lax.rem(me // 2, 2)
    my_z = me // 4
    here = my_x * (2 * line - 1 - my_z) + (1 - my_x) * my_z
    way = 1 - 2 * core

    def block_of(place, on):
        x = place // line
        z = x * (2 * line - 1 - place) + (1 - x) * place
        return (z * 2 + x) * 2 + on

    def wrap(value):
        return lax.rem(value + 2 * turn, turn)

    ahead = block_of(wrap(here + way), core)
    behind = block_of(wrap(here - way), core)
    twin = block_of(here, 1 - core)

    def remote(src, dst, send, recv, to):
        return pltpu.make_async_remote_copy(
            src_ref=src,
            dst_ref=dst,
            send_sem=send,
            recv_sem=recv,
            device_id={"block": to},
            device_id_type=pl.DeviceIdType.MESH,
        )

    def offset(n):
        odd = lax.rem(n, 2)
        return wrap((1 - 2 * odd) * ((n + 1) // 2) * way)

    def hop(n, place, to):
        return [
            remote(buf.at[place, core], buf.at[place, core], ring_send.at[i, n], ring_recv.at[i, n], to)
            for i, buf in enumerate((clips, aux))
        ]

    def swap(off, on):
        place = wrap(here + off)
        return [
            remote(buf.at[place, on], buf.at[place, on], twin_send.at[i, off], twin_recv.at[i, off], twin)
            for i, buf in enumerate((clips, aux))
        ]

    def pass_part(off):
        return remote(given.at[off], taken.at[off], given_send.at[off], taken_recv.at[off], twin)

    def pass_sum(i, off, to):
        return remote(kept.at[off], landed.at[i], sum_send.at[i], sum_recv.at[i], to)

    def start(copies):
        for copy in copies:
            copy.start()

    loads = [
        pltpu.make_async_copy(tokens_ref, clips.at[here, core], load_sem.at[0]),
        pltpu.make_async_copy(aux_ref, aux.at[here, core], load_sem.at[1]),
        pltpu.make_async_copy(gate_ref.at[0], gate_w, load_sem.at[2]),
        pltpu.make_async_copy(up_ref.at[0], up_w, load_sem.at[3]),
        pltpu.make_async_copy(down_ref.at[0], down_w, load_sem.at[4]),
    ]
    start(loads)

    barrier = pltpu.get_barrier_semaphore()
    for other in (ahead, behind, twin):
        pl.semaphore_signal(
            barrier, inc=1, device_id={"block": other}, device_id_type=pl.DeviceIdType.MESH
        )
    pl.semaphore_wait(barrier, 3)

    loads[0].wait()
    loads[1].wait()
    start(hop(1, here, ahead))
    start(hop(2, here, behind))
    start(swap(0, core))
    for load in loads[2:]:
        load.wait()

    scale_d = width ** (-0.5)
    scale_m = mem ** (-0.5)
    eye = lax.broadcasted_iota(jnp.int32, (rows, rows), 0) == lax.broadcasted_iota(
        jnp.int32, (rows, rows), 1
    )

    def column(place, on):
        row = aux[place, on, pl.ds(me, 1), :]
        return jnp.sum(jnp.where(eye, jnp.broadcast_to(row, (rows, rows)), 0.0), axis=1, keepdims=True)

    def work(off):
        place = wrap(here + off)
        x = clips[place].reshape(2 * rows, width)
        hidden = []
        for at in range(0, hidden_width, 256):
            cols = slice(at, min(at + 256, hidden_width))
            g = dot(x, gate_w[:, cols])
            u = dot(x, up_w[:, cols])
            hidden.append((g / (1.0 + jnp.exp(-g)) * u).astype(jnp.bfloat16))
        hidden = jnp.concatenate(hidden, axis=1)
        shares = jnp.concatenate([column(place, 0), column(place, 1)], axis=0)
        for at in range(0, width, 512):
            cols = slice(at, min(at + 512, width))
            out = (dot(hidden, down_w[:, cols]) * shares).astype(jnp.bfloat16)
            out = out.reshape(2, rows, out.shape[1])

            @pl.when(core == 0)
            def _():
                kept[off, :, cols] = out[0]
                given[off, :, cols] = out[1]

            @pl.when(core == 1)
            def _():
                kept[off, :, cols] = out[1]
                given[off, :, cols] = out[0]

        pass_part(off).start()
        scores = (dot(x, keys_ref[...], 1, 1) * scale_d).astype(jnp.bfloat16)
        for on in range(2):
            piece = slice(on * rows, (on + 1) * rows)
            writes[block_of(place, on)] = dot(scores[piece], x[piece], 0, 0) * (1.0 / rows)

    def add_up(off, parts):
        pass_part(off).wait_recv()

        def some(i, _):
            at = pl.ds(pl.multiple_of(i * 16, 16), 16)
            total = kept[off, at, :].astype(jnp.float32) + taken[off, at, :].astype(jnp.float32)
            for part in parts:
                total = total + landed[part, at, :].astype(jnp.float32)
            kept[off, at, :] = total.astype(jnp.bfloat16)
            return 0

        lax.fori_loop(0, rows // 16, some, 0)

    def long_sum(i):
        off = wrap((half - i) * way)
        if i > 0:
            pass_sum(i - 1, off, ahead).wait_recv()
        add_up(off, [i - 1] if i > 0 else [])
        pass_sum(i, off, ahead).start()

    def short_sum(i):
        off = wrap((i - (half - 1)) * way)
        if i > 0:
            pass_sum(half + i - 1, off, behind).wait_recv()
        add_up(off, [half + i - 1] if i > 0 else [])
        pass_sum(half + i, off, behind).start()

    def arrive(n, to):
        off = offset(n)
        place = wrap(here + off)
        for copy in hop(n, place, to):
            copy.wait_recv()

        @pl.when(n + 2 <= turn - 1)
        def _():
            start(hop(n + 2, place, to))

        start(swap(off, core))

    def step(n, _):
        off = offset(n)

        @pl.when(lax.rem(n, 2) == 1)
        def _():
            arrive(n, ahead)

            @pl.when(n + 1 <= turn - 2)
            def _():
                arrive(n + 1, behind)

        for copy in swap(off, 1 - core):
            copy.wait_recv()
        work(off)

        @pl.when(n == turn - 2)
        def _():
            short_sum(0)

        return 0

    lax.fori_loop(0, turn, step, 0)
    long_sum(0)

    def lap(clip, carry):
        place_x = lax.rem(clip // 2, 2)
        place_z = clip // 4
        place = place_x * (2 * line - 1 - place_z) + (1 - place_x) * place_z
        keep = keep_row(aux[place, lax.rem(clip, 2), count:, :])
        longer = keep * state_ref[...] + writes[clip]
        state_ref[...] = longer
        return carry

    def keep_row(block):
        return jnp.concatenate([block[i : i + 1, :] for i in range(block.shape[0])], axis=1)

    state_ref[...] = jnp.zeros((mem, width), jnp.float32)
    lax.fori_loop(0, me, lap, 0)
    read = state_ref[...].astype(jnp.bfloat16)
    lap(me, 0)
    own = clips[here, core]
    scores = (dot(own, read, 1, 1) * scale_d).astype(jnp.bfloat16)
    for at in range(0, width, 512):
        cols = slice(at, min(at + 512, width))
        base[:, cols] = dot(scores, read[:, cols]) * scale_m

    for i in range(1, half):
        if i < half - 1:
            short_sum(i)
        long_sum(i)

    pass_part(0).wait_recv()
    pass_sum(half - 1, 0, ahead).wait_recv()
    pass_sum(2 * half - 2, 0, behind).wait_recv()

    def finish_some(i, _):
        at = pl.ds(pl.multiple_of(i * 16, 16), 16)
        total = kept[0, at, :].astype(jnp.float32) + taken[0, at, :].astype(jnp.float32)
        total = total + landed[half - 1, at, :].astype(jnp.float32)
        total = total + landed[2 * half - 2, at, :].astype(jnp.float32)
        mixed_ref[at, :] = (total + base[at, :]).astype(jnp.bfloat16)
        return 0

    lax.fori_loop(0, rows // 16, finish_some, 0)

    for n in range(1, turn):
        for copy in hop(n, here, ahead):
            copy.wait_send()
    for off in range(turn):
        for copy in swap(off, core):
            copy.wait_send()
        pass_part(off).wait_send()
    for i in range(2 * half - 1):
        pass_sum(i, 0, ahead).wait_send()


def dense(tokens, expert_ids, route_weight, memory_keep, mem_keys, w_gate, w_up, w_down):
    rows, width = tokens.shape
    mem = mem_keys.shape[0]
    hidden = w_gate.shape[2]
    count = lax.axis_size("block")
    turn = count // 2
    hot = expert_ids[None, :, :] == jnp.arange(count, dtype=jnp.int32)[:, None, None]
    shares = jnp.sum(jnp.where(hot, route_weight[None, :, :], 0.0), axis=2)
    aux = jnp.concatenate([shares, memory_keep.reshape(-1, rows)], axis=0)
    bf16, f32 = jnp.bfloat16, jnp.float32
    anywhere = pl.BlockSpec(memory_space=pl.ANY)
    vmem = pl.BlockSpec(memory_space=pltpu.VMEM)
    dma = pltpu.SemaphoreType.DMA
    return pl.pallas_call(
        functools.partial(dense_kernel, count),
        out_shape=(
            jax.ShapeDtypeStruct((rows, width), bf16),
            jax.ShapeDtypeStruct((mem, width), f32),
        ),
        in_specs=[anywhere, anywhere, vmem, anywhere, anywhere, anywhere],
        out_specs=(vmem, vmem),
        scratch_shapes=[
            pltpu.VMEM((turn, 2, rows, width), bf16),
            pltpu.VMEM((turn, 2) + aux.shape, f32),
            pltpu.VMEM((width, hidden), bf16),
            pltpu.VMEM((width, hidden), bf16),
            pltpu.VMEM((hidden, width), bf16),
            pltpu.VMEM((turn, rows, width), bf16),
            pltpu.VMEM((turn, rows, width), bf16),
            pltpu.VMEM((turn, rows, width), bf16),
            pltpu.VMEM((turn - 1, rows, width), bf16),
            pltpu.VMEM((count, mem, width), f32),
            pltpu.VMEM((rows, width), f32),
            dma((5,)),
            dma((2, turn)),
            dma((2, turn)),
            dma((2, turn)),
            dma((2, turn)),
            dma((turn,)),
            dma((turn,)),
            dma((turn - 1,)),
            dma((turn - 1,)),
        ],
        compiler_params=pltpu.CompilerParams(
            collective_id=0, has_side_effects=True, vmem_limit_bytes=56 * 2**20
        ),
        cost_estimate=pl.CostEstimate(
            flops=6 * count * rows * width * hidden, bytes_accessed=2 * 3 * width * hidden, transcendentals=0
        ),
    )(tokens, aux, mem_keys, w_gate, w_up, w_down)


def solution(mesh):
    experts = mesh.shape["block"]

    def shards(tokens, expert_ids, *rest):
        few = experts <= 4 * expert_ids.shape[1]
        return (dense if few else sparse)(tokens, expert_ids, *rest)

    return jax.shard_map(
        shards,
        mesh=mesh,
        in_specs=(
            P(("groups", "block"), None),
            P(("groups", "block"), None),
            P(("groups", "block"), None),
            P(("groups", "block"), None),
            P(),
            P("block", None, None),
            P("block", None, None),
            P("block", None, None),
        ),
        out_specs=(P(("groups", "block"), None), P(("groups", "block"), None)),
        check_vma=False,
    )
```

```python
import functools

import jax
import jax.numpy as jnp
from jax import lax
from jax.experimental import pallas as pl
from jax.experimental.pallas import tpu as pltpu
from jax.sharding import PartitionSpec as P


def prefix(value, axis, join, neutral):
    count, mine = (lax.axis_size(axis), lax.axis_index(axis))
    pieces = jax.tree.map(lambda part: lax.all_gather(part, axis), value)
    subtotal = jax.tree.map(
        lambda part, zero: jnp.full_like(part, 0) + jnp.asarray(zero, part.dtype), value, neutral
    )

    def lap(position, subtotal):
        longer = join(subtotal, jax.tree.map(lambda part: part[position], pieces))
        return jax.tree.map(lambda new, old: jnp.where(position < mine, new, old), longer, subtotal)

    return lax.fori_loop(0, count - 1, lap, subtotal)


def run_expert(received, gate_w, up_w, down_w):
    count, slots, width = received.shape
    flat = received.reshape(count * slots, width)
    gate = jnp.dot(flat, gate_w, preferred_element_type=jnp.float32)
    upper = jnp.dot(flat, up_w, preferred_element_type=jnp.float32)
    hidden = (jax.nn.silu(gate) * upper).astype(jnp.bfloat16)
    produced = jnp.dot(hidden, down_w, preferred_element_type=jnp.float32).astype(jnp.bfloat16)
    return produced.reshape(count, slots, width)


def chain(earlier, later):
    return (earlier[0] * later[0], later[0][None, :] * earlier[1] + later[1])


def sparse_moe(tokens, expert_ids, route_weight, w_gate, w_up, w_down):
    tok_rows, width = tokens.shape
    topk = expert_ids.shape[1]
    experts = lax.axis_size("block")
    capacity = max(2, (3 * tok_rows * topk + 2 * experts - 1) // (2 * experts))
    pairs = expert_ids.reshape(-1)
    onehot = (pairs[:, None] == jnp.arange(experts, dtype=jnp.int32)[None, :]).astype(jnp.int32)
    slot = jnp.sum((jnp.cumsum(onehot, axis=0) - onehot) * onehot, axis=1)
    dest = pairs * capacity + slot
    source_rows = jnp.repeat(tokens, topk, axis=0)
    outgoing = jnp.zeros((experts * capacity, width), jnp.bfloat16).at[dest].set(source_rows)
    outgoing = outgoing.reshape(experts, capacity, width)
    received = lax.all_to_all(outgoing, "block", split_axis=0, concat_axis=0, tiled=True)
    produced = run_expert(received, w_gate[0], w_up[0], w_down[0])
    returned = lax.all_to_all(produced, "block", split_axis=0, concat_axis=0, tiled=True)
    picked = returned.reshape(experts * capacity, width)[dest]
    weighted = picked.astype(jnp.float32).reshape(tok_rows, topk, width) * route_weight[:, :, None]
    return jnp.sum(weighted, axis=1)


def sparse(tokens, expert_ids, route_weight, memory_keep, mem_keys, w_gate, w_up, w_down):
    tok_rows, width = tokens.shape
    moe = sparse_moe(tokens, expert_ids, route_weight, w_gate, w_up, w_down)
    scale_d = width ** (-0.5)
    scores = (jnp.dot(tokens, mem_keys.T, preferred_element_type=jnp.float32) * scale_d).astype(
        jnp.bfloat16
    )
    write = jnp.dot(scores.T, tokens, preferred_element_type=jnp.float32) / tok_rows
    survival_flags = memory_keep[0]
    identity = (jnp.ones_like(survival_flags), jnp.zeros_like(write))
    _, memory_in = prefix((survival_flags, write), "block", chain, identity)
    memory_state = survival_flags[None, :] * memory_in + write
    return finish(tokens, moe, memory_in), memory_state


def finish(tokens, moe, memory_in):
    scale_d = tokens.shape[1] ** (-0.5)
    scale_m = memory_in.shape[0] ** (-0.5)
    memory_read = memory_in.astype(jnp.bfloat16)
    read_scores = (
        jnp.dot(tokens, memory_read.T, preferred_element_type=jnp.float32) * scale_d
    ).astype(jnp.bfloat16)
    recall = jnp.dot(read_scores, memory_read, preferred_element_type=jnp.float32) * scale_m
    return (moe.astype(jnp.float32) + recall).astype(jnp.bfloat16)


def dot(a, b, ca=1, cb=0):
    return lax.dot_general(a, b, (((ca,), (cb,)), ((), ())), preferred_element_type=jnp.float32)


def dense_kernel(
    count,
    tokens_ref,
    aux_ref,
    keys_ref,
    gate_ref,
    up_ref,
    down_ref,
    mixed_ref,
    state_ref,
    clips,
    aux,
    gate_w,
    up_w,
    down_w,
    parts,
    taken,
    landed,
    base,
    load_sem,
    ring_send,
    ring_recv,
    twin_send,
    twin_recv,
    part_send,
    part_recv,
    sum_send,
    sum_recv,
):
    turn = count // 2
    line = turn // 2
    far = turn // 2
    rows, width = tokens_ref.shape
    piece = rows // 2
    hidden_width = gate_w.shape[1]
    mem = keys_ref.shape[0]
    me = lax.axis_index("block")
    core = lax.rem(me, 2)
    way = 1 - 2 * core

    def place_of(block):
        x = lax.rem(block // 2, 2)
        z = block // 4
        return x * (2 * line - 1 - z) + (1 - x) * z

    def block_of(place, on):
        x = place // line
        z = x * (2 * line - 1 - place) + (1 - x) * place
        return (z * 2 + x) * 2 + on

    def wrap(value):
        return lax.rem(value + 2 * turn, turn)

    here = place_of(me)
    ahead = block_of(wrap(here + way), core)
    behind = block_of(wrap(here - way), core)
    twin = block_of(here, 1 - core)

    def span(h):
        if isinstance(h, int):
            return pl.ds(h * piece, piece)
        return pl.ds(pl.multiple_of(h * piece, piece), piece)

    def remote(src, dst, send, recv, to):
        return pltpu.make_async_remote_copy(
            src_ref=src,
            dst_ref=dst,
            send_sem=send,
            recv_sem=recv,
            device_id={"block": to},
            device_id_type=pl.DeviceIdType.MESH,
        )

    def offset(n):
        odd = lax.rem(n, 2)
        return wrap((1 - 2 * odd) * ((n + 1) // 2) * way)

    def hop(n, h, place, to, own=False):
        dst = clips.at[place, core, span(h)]
        src = tokens_ref.at[span(h)] if own else dst
        return remote(src, dst, ring_send.at[h, n], ring_recv.at[h, n], to)

    def hop_aux(n, place, to, own=False):
        dst = aux.at[place, core]
        src = aux_ref if own else dst
        return remote(src, dst, ring_send.at[2, n], ring_recv.at[2, n], to)

    def swap(off, h, on, own=False):
        dst = clips.at[wrap(here + off), on, span(h)]
        src = tokens_ref.at[span(h)] if own else dst
        return remote(src, dst, twin_send.at[h, off], twin_recv.at[h, off], twin)

    def swap_aux(off, on, own=False):
        dst = aux.at[wrap(here + off), on]
        src = aux_ref if own else dst
        return remote(src, dst, twin_send.at[2, off], twin_recv.at[2, off], twin)

    def pass_part(off, h):
        return remote(
            parts.at[1 - core, off, span(h)],
            taken.at[off, span(h)],
            part_send.at[h, off],
            part_recv.at[h, off],
            twin,
        )

    def pass_sum(i, h, off, to):
        return remote(
            parts.at[core, off, span(h)],
            landed.at[i, span(h)],
            sum_send.at[h, i],
            sum_recv.at[h, i],
            to,
        )

    loads = [
        pltpu.make_async_copy(tokens_ref, clips.at[here, core], load_sem.at[0]),
        pltpu.make_async_copy(aux_ref, aux.at[here, core], load_sem.at[1]),
        pltpu.make_async_copy(gate_ref.at[0], gate_w, load_sem.at[2]),
        pltpu.make_async_copy(up_ref.at[0], up_w, load_sem.at[3]),
        pltpu.make_async_copy(down_ref.at[0], down_w, load_sem.at[4]),
    ]

    barrier = pltpu.get_barrier_semaphore()
    for other in (ahead, behind, twin):
        pl.semaphore_signal(
            barrier, inc=1, device_id={"block": other}, device_id_type=pl.DeviceIdType.MESH
        )
    for load in loads:
        load.start()
    pl.semaphore_wait(barrier, 3)

    for h in range(2):
        hop(1, h, here, ahead, True).start()
        hop(2, h, here, behind, True).start()
        if h == 0:
            hop_aux(1, here, ahead, True).start()
            hop_aux(2, here, behind, True).start()
        swap(0, h, core, True).start()
    swap_aux(0, core, True).start()
    for load in loads:
        load.wait()

    scale_d = width ** (-0.5)
    scale_m = mem ** (-0.5)
    down_row = lax.broadcasted_iota(jnp.int32, (piece, rows), 0)
    along = lax.broadcasted_iota(jnp.int32, (piece, rows), 1)

    def column(place, on, h):
        row = jnp.broadcast_to(aux[place, on, pl.ds(me, 1), :], (piece, rows))
        picked = jnp.where(down_row + h * piece == along, row, 0.0)
        return jnp.sum(picked, axis=1, keepdims=True)

    def work(halves):
        pieces = [(off, h, on) for off, h in halves for on in range(2)]
        x = jnp.concatenate([clips[wrap(here + off), on, span(h), :] for off, h, on in pieces], axis=0)
        hidden = []
        for at in range(0, hidden_width, 256):
            cols = slice(at, min(at + 256, hidden_width))
            g = dot(x, gate_w[:, cols])
            u = dot(x, up_w[:, cols])
            hidden.append((g / (1.0 + jnp.exp(-g)) * u).astype(jnp.bfloat16))
        hidden = jnp.concatenate(hidden, axis=1)
        shares = jnp.concatenate([column(wrap(here + off), on, h) for off, h, on in pieces], axis=0)
        for at in range(0, width, 512):
            cols = slice(at, min(at + 512, width))
            out = (dot(hidden, down_w[:, cols]) * shares).astype(jnp.bfloat16)
            for j, (off, h, on) in enumerate(pieces):
                parts[on, off, span(h), cols] = out[j * piece : (j + 1) * piece]
        for off, h in halves:
            pass_part(off, h).start()

    def add_up(off, h, part):
        pass_part(off, h).wait_recv()

        def some(i, _):
            at = pl.ds(pl.multiple_of(h * piece + i * 16, 16), 16)
            total = parts[core, off, at, :].astype(jnp.float32)
            total = total + taken[off, at, :].astype(jnp.float32)
            if part is not None:
                total = total + landed[part, at, :].astype(jnp.float32)
            parts[core, off, at, :] = total.astype(jnp.bfloat16)
            return 0

        lax.fori_loop(0, piece // 16, some, 0)

    def long_sum(i, h):
        off = wrap((far - i) * way)
        if i > 0:
            pass_sum(i - 1, h, off, ahead).wait_recv()
        add_up(off, h, i - 1 if i > 0 else None)
        pass_sum(i, h, off, ahead).start()

    def short_sum(i, h):
        off = wrap((i - (far - 1)) * way)
        if i > 0:
            pass_sum(far + i - 1, h, off, behind).wait_recv()
        add_up(off, h, far + i - 1 if i > 0 else None)
        pass_sum(far + i, h, off, behind).start()

    def arrive(n, h, to):
        off = offset(n)
        place = wrap(here + off)
        hop(n, h, place, to).wait_recv()

        @pl.when(n + 2 <= turn - 1)
        def _():
            hop(n + 2, h, place, to).start()

        swap(off, h, core).start()

        @pl.when(h == 0)
        def _():
            hop_aux(n, place, to).wait_recv()

            @pl.when(n + 2 <= turn - 1)
            def _():
                hop_aux(n + 2, place, to).start()

            swap_aux(off, core).start()

    def met(off, h):
        swap(off, h, 1 - core).wait_recv()

        @pl.when(h == 0)
        def _():
            swap_aux(off, 1 - core).wait_recv()

    def step(t, _):
        k = (t + 1) // 2
        edge = (t == 0) | (t == turn - 1)
        h = lax.rem(t + 1, 2)
        off_a = wrap(-k * way)
        off_b = wrap(k * way)
        h_a = jnp.where(edge, 0, h)
        h_b = jnp.where(edge, 1, h)

        @pl.when(t == turn - 1)
        def _():
            short_sum(0, 1)

        @pl.when(t > 0)
        def _():
            arrive(2 * k - 1, h_a, ahead)

            @pl.when(t < turn - 1)
            def _():
                arrive(2 * k, h_b, behind)

            @pl.when(t == turn - 1)
            def _():
                arrive(2 * k - 1, h_b, ahead)

        @pl.when(t == turn - 2)
        def _():
            short_sum(0, 0)

        met(off_a, h_a)
        met(off_b, h_b)
        work([(off_a, h_a), (off_b, h_b)])
        return 0

    lax.fori_loop(0, turn, step, 0)
    long_sum(0, 0)
    long_sum(0, 1)

    def keep_row(clip):
        block = aux[place_of(clip), lax.rem(clip, 2), count:, :]
        return jnp.concatenate([block[i : i + 1, :] for i in range(block.shape[0])], axis=1)

    def remember(clip):
        x = clips[place_of(clip), lax.rem(clip, 2)]
        scores = (dot(x, keys_ref[...], 1, 1) * scale_d).astype(jnp.bfloat16)
        write = dot(scores, x, 0, 0) * (1.0 / rows)
        state_ref[...] = keep_row(clip) * state_ref[...] + write

    def lap(clip, _):
        @pl.when(clip < me)
        def _():
            remember(clip)

        return 0

    def recall():
        read = state_ref[...].astype(jnp.bfloat16)
        remember(me)
        scores = (dot(clips[here, core], read, 1, 1) * scale_d).astype(jnp.bfloat16)
        for at in range(0, width, 512):
            cols = slice(at, min(at + 512, width))
            base[:, cols] = dot(scores, read[:, cols]) * scale_m

    state_ref[...] = jnp.zeros((mem, width), jnp.float32)
    gaps = 2 * (far - 2)
    share = -(-count // gaps)
    gap = 0
    for i in range(1, far):
        for h in range(2):
            if gap < gaps:
                lax.fori_loop(gap * share, min((gap + 1) * share, count), lap, 0)
            elif gap == gaps:
                recall()
            gap += 1
            if i < far - 1:
                short_sum(i, h)
            long_sum(i, h)

    for h in range(2):
        pass_part(0, h).wait_recv()
        pass_sum(2 * far - 2, h, 0, behind).wait_recv()
        pass_sum(far - 1, h, 0, ahead).wait_recv()

        def finish_some(i, _):
            at = pl.ds(pl.multiple_of(h * piece + i * 16, 16), 16)
            total = parts[core, 0, at, :].astype(jnp.float32) + taken[0, at, :].astype(jnp.float32)
            total = total + landed[far - 1, at, :].astype(jnp.float32)
            total = total + landed[2 * far - 2, at, :].astype(jnp.float32)
            mixed_ref[at, :] = (total + base[at, :]).astype(jnp.bfloat16)
            return 0

        lax.fori_loop(0, piece // 16, finish_some, 0)

    for n in range(1, turn):
        hop_aux(n, here, ahead).wait_send()
        for h in range(2):
            hop(n, h, here, ahead).wait_send()
    for off in range(turn):
        swap_aux(off, core).wait_send()
        for h in range(2):
            swap(off, h, core).wait_send()
            pass_part(off, h).wait_send()
    for i in range(2 * far - 1):
        for h in range(2):
            pass_sum(i, h, 0, ahead).wait_send()


def dense(tokens, expert_ids, route_weight, memory_keep, mem_keys, w_gate, w_up, w_down):
    rows, width = tokens.shape
    mem = mem_keys.shape[0]
    hidden = w_gate.shape[2]
    count = lax.axis_size("block")
    turn = count // 2
    hot = expert_ids[None, :, :] == jnp.arange(count, dtype=jnp.int32)[:, None, None]
    shares = jnp.sum(jnp.where(hot, route_weight[None, :, :], 0.0), axis=2)
    aux = jnp.concatenate([shares, memory_keep.reshape(-1, rows)], axis=0)
    bf16, f32 = jnp.bfloat16, jnp.float32
    anywhere = pl.BlockSpec(memory_space=pl.ANY)
    vmem = pl.BlockSpec(memory_space=pltpu.VMEM)
    dma = pltpu.SemaphoreType.DMA
    return pl.pallas_call(
        functools.partial(dense_kernel, count),
        out_shape=(
            jax.ShapeDtypeStruct((rows, width), bf16),
            jax.ShapeDtypeStruct((mem, width), f32),
        ),
        in_specs=[anywhere, anywhere, vmem, anywhere, anywhere, anywhere],
        out_specs=(vmem, vmem),
        scratch_shapes=[
            pltpu.VMEM((turn, 2, rows, width), bf16),
            pltpu.VMEM((turn, 2) + aux.shape, f32),
            pltpu.VMEM((width, hidden), bf16),
            pltpu.VMEM((width, hidden), bf16),
            pltpu.VMEM((hidden, width), bf16),
            pltpu.VMEM((2, turn, rows, width), bf16),
            pltpu.VMEM((turn, rows, width), bf16),
            pltpu.VMEM((turn - 1, rows, width), bf16),
            pltpu.VMEM((rows, width), f32),
            dma((5,)),
            dma((3, turn)),
            dma((3, turn)),
            dma((3, turn)),
            dma((3, turn)),
            dma((2, turn)),
            dma((2, turn)),
            dma((2, turn - 1)),
            dma((2, turn - 1)),
        ],
        compiler_params=pltpu.CompilerParams(
            collective_id=0, has_side_effects=True, vmem_limit_bytes=56 * 2**20
        ),
        cost_estimate=pl.CostEstimate(
            flops=6 * count * rows * width * hidden, bytes_accessed=2 * 3 * width * hidden, transcendentals=0
        ),
    )(tokens, aux, mem_keys, w_gate, w_up, w_down)


def solution(mesh):
    experts = mesh.shape["block"]

    def shards(tokens, expert_ids, *rest):
        few = experts <= 4 * expert_ids.shape[1]
        return (dense if few else sparse)(tokens, expert_ids, *rest)

    return jax.shard_map(
        shards,
        mesh=mesh,
        in_specs=(
            P(("groups", "block"), None),
            P(("groups", "block"), None),
            P(("groups", "block"), None),
            P(("groups", "block"), None),
            P(),
            P("block", None, None),
            P("block", None, None),
            P("block", None, None),
        ),
        out_specs=(P(("groups", "block"), None), P(("groups", "block"), None)),
        check_vma=False,
    )
```

```python
import functools

import jax
import jax.numpy as jnp
from jax import lax
from jax.experimental import pallas as pl
from jax.experimental.pallas import tpu as pltpu
from jax.sharding import PartitionSpec as P


def prefix(value, axis, join, neutral):
    count, mine = (lax.axis_size(axis), lax.axis_index(axis))
    pieces = jax.tree.map(lambda part: lax.all_gather(part, axis), value)
    subtotal = jax.tree.map(
        lambda part, zero: jnp.full_like(part, 0) + jnp.asarray(zero, part.dtype), value, neutral
    )

    def lap(position, subtotal):
        longer = join(subtotal, jax.tree.map(lambda part: part[position], pieces))
        return jax.tree.map(lambda new, old: jnp.where(position < mine, new, old), longer, subtotal)

    return lax.fori_loop(0, count - 1, lap, subtotal)


def run_expert(received, gate_w, up_w, down_w):
    count, slots, width = received.shape
    flat = received.reshape(count * slots, width)
    gate = jnp.dot(flat, gate_w, preferred_element_type=jnp.float32)
    upper = jnp.dot(flat, up_w, preferred_element_type=jnp.float32)
    hidden = (jax.nn.silu(gate) * upper).astype(jnp.bfloat16)
    produced = jnp.dot(hidden, down_w, preferred_element_type=jnp.float32).astype(jnp.bfloat16)
    return produced.reshape(count, slots, width)


def chain(earlier, later):
    return (earlier[0] * later[0], later[0][None, :] * earlier[1] + later[1])


def sparse_moe(tokens, expert_ids, route_weight, w_gate, w_up, w_down):
    tok_rows, width = tokens.shape
    topk = expert_ids.shape[1]
    experts = lax.axis_size("block")
    capacity = max(2, (3 * tok_rows * topk + 2 * experts - 1) // (2 * experts))
    pairs = expert_ids.reshape(-1)
    onehot = (pairs[:, None] == jnp.arange(experts, dtype=jnp.int32)[None, :]).astype(jnp.int32)
    slot = jnp.sum((jnp.cumsum(onehot, axis=0) - onehot) * onehot, axis=1)
    dest = pairs * capacity + slot
    source_rows = jnp.repeat(tokens, topk, axis=0)
    outgoing = jnp.zeros((experts * capacity, width), jnp.bfloat16).at[dest].set(source_rows)
    outgoing = outgoing.reshape(experts, capacity, width)
    received = lax.all_to_all(outgoing, "block", split_axis=0, concat_axis=0, tiled=True)
    produced = run_expert(received, w_gate[0], w_up[0], w_down[0])
    returned = lax.all_to_all(produced, "block", split_axis=0, concat_axis=0, tiled=True)
    picked = returned.reshape(experts * capacity, width)[dest]
    weighted = picked.astype(jnp.float32).reshape(tok_rows, topk, width) * route_weight[:, :, None]
    return jnp.sum(weighted, axis=1)


def sparse(tokens, expert_ids, route_weight, memory_keep, mem_keys, w_gate, w_up, w_down):
    tok_rows, width = tokens.shape
    moe = sparse_moe(tokens, expert_ids, route_weight, w_gate, w_up, w_down)
    scale_d = width ** (-0.5)
    scores = (jnp.dot(tokens, mem_keys.T, preferred_element_type=jnp.float32) * scale_d).astype(
        jnp.bfloat16
    )
    write = jnp.dot(scores.T, tokens, preferred_element_type=jnp.float32) / tok_rows
    survival_flags = memory_keep[0]
    identity = (jnp.ones_like(survival_flags), jnp.zeros_like(write))
    _, memory_in = prefix((survival_flags, write), "block", chain, identity)
    memory_state = survival_flags[None, :] * memory_in + write
    return finish(tokens, moe, memory_in), memory_state


def finish(tokens, moe, memory_in):
    scale_d = tokens.shape[1] ** (-0.5)
    scale_m = memory_in.shape[0] ** (-0.5)
    memory_read = memory_in.astype(jnp.bfloat16)
    read_scores = (
        jnp.dot(tokens, memory_read.T, preferred_element_type=jnp.float32) * scale_d
    ).astype(jnp.bfloat16)
    recall = jnp.dot(read_scores, memory_read, preferred_element_type=jnp.float32) * scale_m
    return (moe.astype(jnp.float32) + recall).astype(jnp.bfloat16)


def dot(a, b, ca=1, cb=0):
    return lax.dot_general(a, b, (((ca,), (cb,)), ((), ())), preferred_element_type=jnp.float32)


def dense_kernel(
    count,
    tokens_ref,
    ids_ref,
    weight_ref,
    keep_ref,
    keys_ref,
    gate_ref,
    up_ref,
    down_ref,
    mixed_ref,
    state_ref,
    clips,
    aux,
    ids,
    weight,
    keys,
    state,
    mixed,
    gate_w,
    up_w,
    down_w,
    parts,
    taken,
    landed,
    base,
    load_sem,
    out_sem,
    ring_send,
    ring_recv,
    twin_send,
    twin_recv,
    part_send,
    part_recv,
    sum_send,
    sum_recv,
):
    turn = count // 2
    line = turn // 2
    far = turn // 2
    rows, width = tokens_ref.shape
    piece = rows // 2
    hidden_width = gate_w.shape[1]
    mem = keys.shape[0]
    me = lax.axis_index("block")
    core = lax.rem(me, 2)
    way = 1 - 2 * core

    def place_of(block):
        x = lax.rem(block // 2, 2)
        z = block // 4
        return x * (2 * line - 1 - z) + (1 - x) * z

    def block_of(place, on):
        x = place // line
        z = x * (2 * line - 1 - place) + (1 - x) * place
        return (z * 2 + x) * 2 + on

    def wrap(value):
        return lax.rem(value + 2 * turn, turn)

    here = place_of(me)
    ahead = block_of(wrap(here + way), core)
    behind = block_of(wrap(here - way), core)
    twin = block_of(here, 1 - core)

    def span(h):
        if isinstance(h, int):
            return pl.ds(h * piece, piece)
        return pl.ds(pl.multiple_of(h * piece, piece), piece)

    def remote(src, dst, send, recv, to):
        return pltpu.make_async_remote_copy(
            src_ref=src,
            dst_ref=dst,
            send_sem=send,
            recv_sem=recv,
            device_id={"block": to},
            device_id_type=pl.DeviceIdType.MESH,
        )

    def offset(n):
        odd = lax.rem(n, 2)
        return wrap((1 - 2 * odd) * ((n + 1) // 2) * way)

    def hop(n, h, place, to, own=False):
        dst = clips.at[place, core, span(h)]
        src = tokens_ref.at[span(h)] if own else dst
        return remote(src, dst, ring_send.at[h, n], ring_recv.at[h, n], to)

    def hop_aux(n, place, to):
        both = aux.at[place, core]
        return remote(both, both, ring_send.at[2, n], ring_recv.at[2, n], to)

    def swap(off, h, on, own=False):
        dst = clips.at[wrap(here + off), on, span(h)]
        src = tokens_ref.at[span(h)] if own else dst
        return remote(src, dst, twin_send.at[h, off], twin_recv.at[h, off], twin)

    def swap_aux(off, on):
        both = aux.at[wrap(here + off), on]
        return remote(both, both, twin_send.at[2, off], twin_recv.at[2, off], twin)

    def pass_part(off, h):
        return remote(
            parts.at[1 - core, off, span(h)],
            taken.at[off, span(h)],
            part_send.at[h, off],
            part_recv.at[h, off],
            twin,
        )

    def pass_sum(i, h, off, to):
        return remote(
            parts.at[core, off, span(h)],
            landed.at[i, span(h)],
            sum_send.at[h, i],
            sum_recv.at[h, i],
            to,
        )

    loads = [
        pltpu.make_async_copy(src, dst, load_sem.at[i])
        for i, (src, dst) in enumerate(
            (
                (ids_ref, ids),
                (weight_ref, weight),
                (keep_ref, aux.at[here, core, pl.ds(count, width // rows)]),
                (tokens_ref, clips.at[here, core]),
                (gate_ref.at[0], gate_w),
                (up_ref.at[0], up_w),
                (down_ref.at[0], down_w),
                (keys_ref, keys),
            )
        )
    ]

    barrier = pltpu.get_barrier_semaphore()
    for other in (ahead, behind, twin):
        pl.semaphore_signal(
            barrier, inc=1, device_id={"block": other}, device_id_type=pl.DeviceIdType.MESH
        )
    for load in loads:
        load.start()
    pl.semaphore_wait(barrier, 3)

    for h in range(2):
        hop(1, h, here, ahead, True).start()
        hop(2, h, here, behind, True).start()
        swap(0, h, core, True).start()
        if h == 0:
            for load in loads[:3]:
                load.wait()
            for e in range(count):
                named = jnp.where(ids[...] == e, weight[...], 0.0)
                aux[here, core, e : e + 1, :] = jnp.sum(named, axis=0, keepdims=True)
            hop_aux(1, here, ahead).start()
            hop_aux(2, here, behind).start()
            swap_aux(0, core).start()

    scale_d = width ** (-0.5)
    scale_m = mem ** (-0.5)
    down_row = lax.broadcasted_iota(jnp.int32, (piece, rows), 0)
    along = lax.broadcasted_iota(jnp.int32, (piece, rows), 1)

    def column(place, on, h):
        row = jnp.broadcast_to(aux[place, on, pl.ds(me, 1), :], (piece, rows))
        picked = jnp.where(down_row + h * piece == along, row, 0.0)
        return jnp.sum(picked, axis=1, keepdims=True)

    def work(halves):
        pieces = [(off, h, on) for off, h in halves for on in range(2)]
        x = jnp.concatenate([clips[wrap(here + off), on, span(h), :] for off, h, on in pieces], axis=0)
        hidden = []
        for at in range(0, hidden_width, 256):
            cols = slice(at, min(at + 256, hidden_width))
            g = dot(x, gate_w[:, cols])
            u = dot(x, up_w[:, cols])
            hidden.append((g / (1.0 + jnp.exp(-g)) * u).astype(jnp.bfloat16))
        hidden = jnp.concatenate(hidden, axis=1)
        shares = jnp.concatenate([column(wrap(here + off), on, h) for off, h, on in pieces], axis=0)
        for at in range(0, width, 512):
            cols = slice(at, min(at + 512, width))
            out = (dot(hidden, down_w[:, cols]) * shares).astype(jnp.bfloat16)
            for j, (off, h, on) in enumerate(pieces):
                parts[on, off, span(h), cols] = out[j * piece : (j + 1) * piece]
        for off, h in halves:
            pass_part(off, h).start()

    def add_up(off, h, part):
        pass_part(off, h).wait_recv()

        def some(i, _):
            at = pl.ds(pl.multiple_of(h * piece + i * 16, 16), 16)
            total = parts[core, off, at, :].astype(jnp.float32)
            total = total + taken[off, at, :].astype(jnp.float32)
            if part is not None:
                total = total + landed[part, at, :].astype(jnp.float32)
            parts[core, off, at, :] = total.astype(jnp.bfloat16)
            return 0

        lax.fori_loop(0, piece // 16, some, 0)

    def long_sum(i, h):
        off = wrap((far - i) * way)
        if i > 0:
            pass_sum(i - 1, h, off, ahead).wait_recv()
        add_up(off, h, i - 1 if i > 0 else None)
        pass_sum(i, h, off, ahead).start()

    def short_sum(i, h):
        off = wrap((i - (far - 1)) * way)
        if i > 0:
            pass_sum(far + i - 1, h, off, behind).wait_recv()
        add_up(off, h, far + i - 1 if i > 0 else None)
        pass_sum(far + i, h, off, behind).start()

    def arrive(n, h, to):
        off = offset(n)
        place = wrap(here + off)
        hop(n, h, place, to).wait_recv()

        @pl.when(n + 2 <= turn - 1)
        def _():
            hop(n + 2, h, place, to).start()

        swap(off, h, core).start()

        @pl.when(h == 0)
        def _():
            hop_aux(n, place, to).wait_recv()

            @pl.when(n + 2 <= turn - 1)
            def _():
                hop_aux(n + 2, place, to).start()

            swap_aux(off, core).start()

    def met(off, h):
        swap(off, h, 1 - core).wait_recv()

        @pl.when(h == 0)
        def _():
            swap_aux(off, 1 - core).wait_recv()

    def step(t, _):
        k = (t + 1) // 2
        edge = (t == 0) | (t == turn - 1)
        h = lax.rem(t + 1, 2)
        off_a = wrap(-k * way)
        off_b = wrap(k * way)
        h_a = jnp.where(edge, 0, h)
        h_b = jnp.where(edge, 1, h)

        @pl.when(t == 0)
        def _():
            for load in loads[3:]:
                load.wait()

        @pl.when(t == turn - 1)
        def _():
            short_sum(0, 1)

        @pl.when(t > 0)
        def _():
            arrive(2 * k - 1, h_a, ahead)

            @pl.when(t < turn - 1)
            def _():
                arrive(2 * k, h_b, behind)

            @pl.when(t == turn - 1)
            def _():
                arrive(2 * k - 1, h_b, ahead)

        @pl.when(t == turn - 2)
        def _():
            short_sum(0, 0)

        met(off_a, h_a)
        met(off_b, h_b)
        work([(off_a, h_a), (off_b, h_b)])
        return 0

    lax.fori_loop(0, turn, step, 0)
    short_sum(1, 0)
    long_sum(0, 0)
    long_sum(0, 1)
    short_sum(1, 1)

    def keep_row(clip):
        block = aux[place_of(clip), lax.rem(clip, 2), count:, :]
        return jnp.concatenate([block[i : i + 1, :] for i in range(block.shape[0])], axis=1)

    def remember(clip):
        x = clips[place_of(clip), lax.rem(clip, 2)]
        scores = (dot(x, keys[...], 1, 1) * scale_d).astype(jnp.bfloat16)
        write = dot(scores, x, 0, 0) * (1.0 / rows)
        state[...] = keep_row(clip) * state[...] + write

    def lap(clip, _):
        @pl.when(clip < me)
        def _():
            remember(clip)

        return 0

    def recall():
        read = state[...].astype(jnp.bfloat16)
        remember(me)
        scores = (dot(clips[here, core], read, 1, 1) * scale_d).astype(jnp.bfloat16)
        for at in range(0, width, 512):
            cols = slice(at, min(at + 512, width))
            base[:, cols] = dot(scores, read[:, cols]) * scale_m

    state[...] = jnp.zeros((mem, width), jnp.float32)
    gaps = 2 * (far - 2)
    share = -(-count // gaps)

    def fill(gap):
        if gap < gaps:
            lax.fori_loop(gap * share, min((gap + 1) * share, count), lap, 0)
        elif gap == gaps:
            recall()
            pltpu.make_async_copy(state, state_ref, out_sem.at[2]).start()

    fill(0)
    for i in range(1, far):
        for h in range(2):
            if i < far - 2:
                short_sum(i + 1, h)
            long_sum(i, h)
            fill(2 * (i - 1) + h + 1)

    def ready(h):
        return pltpu.make_async_copy(mixed.at[span(h)], mixed_ref.at[span(h)], out_sem.at[h])

    for h in range(2):
        pass_part(0, h).wait_recv()
        pass_sum(2 * far - 2, h, 0, behind).wait_recv()
        pass_sum(far - 1, h, 0, ahead).wait_recv()

        def finish_some(i, _):
            at = pl.ds(pl.multiple_of(h * piece + i * 16, 16), 16)
            total = parts[core, 0, at, :].astype(jnp.float32) + taken[0, at, :].astype(jnp.float32)
            total = total + landed[far - 1, at, :].astype(jnp.float32)
            total = total + landed[2 * far - 2, at, :].astype(jnp.float32)
            mixed[at, :] = (total + base[at, :]).astype(jnp.bfloat16)
            return 0

        lax.fori_loop(0, piece // 16, finish_some, 0)
        ready(h).start()

    for n in range(1, turn):
        hop_aux(n, here, ahead).wait_send()
        for h in range(2):
            hop(n, h, here, ahead).wait_send()
    for off in range(turn):
        swap_aux(off, core).wait_send()
        for h in range(2):
            swap(off, h, core).wait_send()
            pass_part(off, h).wait_send()
    for i in range(2 * far - 1):
        for h in range(2):
            pass_sum(i, h, 0, ahead).wait_send()
    pltpu.make_async_copy(state, state_ref, out_sem.at[2]).wait()
    for h in range(2):
        ready(h).wait()


def settle_kernel(mixed_in, state_in, mixed_ref, state_ref, mixed, state, sem):
    ways = ((mixed_in, mixed, mixed_ref), (state_in, state, state_ref))
    into = [pltpu.make_async_copy(src, mid, sem.at[0, i]) for i, (src, mid, _) in enumerate(ways)]
    out = [pltpu.make_async_copy(mid, dst, sem.at[1, i]) for i, (_, mid, dst) in enumerate(ways)]
    for copy in into:
        copy.start()
    for first, second in zip(into, out):
        first.wait()
        second.start()
    for copy in out:
        copy.wait()


def dense(tokens, expert_ids, route_weight, memory_keep, mem_keys, w_gate, w_up, w_down):
    rows, width = tokens.shape
    topk = expert_ids.shape[1]
    mem = mem_keys.shape[0]
    hidden = w_gate.shape[2]
    count = lax.axis_size("block")
    turn = count // 2
    bf16, f32 = jnp.bfloat16, jnp.float32
    anywhere = pl.BlockSpec(memory_space=pl.ANY)
    dma = pltpu.SemaphoreType.DMA
    shapes = (
        jax.ShapeDtypeStruct((rows, width), bf16),
        jax.ShapeDtypeStruct((mem, width), f32),
    )
    results = pl.pallas_call(
        functools.partial(dense_kernel, count),
        out_shape=shapes,
        in_specs=[anywhere] * 8,
        out_specs=(anywhere, anywhere),
        scratch_shapes=[
            pltpu.VMEM((turn, 2, rows, width), bf16),
            pltpu.VMEM((turn, 2, count + width // rows, rows), f32),
            pltpu.VMEM((topk, rows), jnp.int32),
            pltpu.VMEM((topk, rows), f32),
            pltpu.VMEM((mem, width), bf16),
            pltpu.VMEM((mem, width), f32),
            pltpu.VMEM((rows, width), bf16),
            pltpu.VMEM((width, hidden), bf16),
            pltpu.VMEM((width, hidden), bf16),
            pltpu.VMEM((hidden, width), bf16),
            pltpu.VMEM((2, turn, rows, width), bf16),
            pltpu.VMEM((turn, rows, width), bf16),
            pltpu.VMEM((turn - 1, rows, width), bf16),
            pltpu.VMEM((rows, width), f32),
            dma((8,)),
            dma((3,)),
            dma((3, turn)),
            dma((3, turn)),
            dma((3, turn)),
            dma((3, turn)),
            dma((2, turn)),
            dma((2, turn)),
            dma((2, turn - 1)),
            dma((2, turn - 1)),
        ],
        compiler_params=pltpu.CompilerParams(
            collective_id=0, has_side_effects=True, vmem_limit_bytes=56 * 2**20
        ),
        cost_estimate=pl.CostEstimate(
            flops=6 * count * rows * width * hidden, bytes_accessed=2 * 3 * width * hidden, transcendentals=0
        ),
    )(
        tokens,
        expert_ids.T,
        route_weight.T,
        memory_keep.reshape(-1, rows),
        mem_keys,
        w_gate,
        w_up,
        w_down,
    )
    return pl.pallas_call(
        settle_kernel,
        out_shape=shapes,
        in_specs=[anywhere] * 2,
        out_specs=(anywhere, anywhere),
        scratch_shapes=[pltpu.VMEM((rows, width), bf16), pltpu.VMEM((mem, width), f32), dma((2, 2))],
    )(*results)


def solution(mesh):
    experts = mesh.shape["block"]

    def shards(tokens, expert_ids, *rest):
        few = experts <= 4 * expert_ids.shape[1]
        return (dense if few else sparse)(tokens, expert_ids, *rest)

    return jax.shard_map(
        shards,
        mesh=mesh,
        in_specs=(
            P(("groups", "block"), None),
            P(("groups", "block"), None),
            P(("groups", "block"), None),
            P(("groups", "block"), None),
            P(),
            P("block", None, None),
            P("block", None, None),
            P("block", None, None),
        ),
        out_specs=(P(("groups", "block"), None), P(("groups", "block"), None)),
        check_vma=False,
    )
```

```python
import functools

import jax
import jax.numpy as jnp
from jax import lax
from jax.experimental import pallas as pl
from jax.experimental.pallas import tpu as pltpu
from jax.sharding import PartitionSpec as P


def prefix(value, axis, join, neutral):
    count, mine = (lax.axis_size(axis), lax.axis_index(axis))
    pieces = jax.tree.map(lambda part: lax.all_gather(part, axis), value)
    subtotal = jax.tree.map(
        lambda part, zero: jnp.full_like(part, 0) + jnp.asarray(zero, part.dtype), value, neutral
    )

    def lap(position, subtotal):
        longer = join(subtotal, jax.tree.map(lambda part: part[position], pieces))
        return jax.tree.map(lambda new, old: jnp.where(position < mine, new, old), longer, subtotal)

    return lax.fori_loop(0, count - 1, lap, subtotal)


def run_expert(received, gate_w, up_w, down_w):
    count, slots, width = received.shape
    flat = received.reshape(count * slots, width)
    gate = jnp.dot(flat, gate_w, preferred_element_type=jnp.float32)
    upper = jnp.dot(flat, up_w, preferred_element_type=jnp.float32)
    hidden = (jax.nn.silu(gate) * upper).astype(jnp.bfloat16)
    produced = jnp.dot(hidden, down_w, preferred_element_type=jnp.float32).astype(jnp.bfloat16)
    return produced.reshape(count, slots, width)


def chain(earlier, later):
    return (earlier[0] * later[0], later[0][None, :] * earlier[1] + later[1])


def sparse_moe(tokens, expert_ids, route_weight, w_gate, w_up, w_down):
    tok_rows, width = tokens.shape
    topk = expert_ids.shape[1]
    experts = lax.axis_size("block")
    capacity = max(2, (3 * tok_rows * topk + 2 * experts - 1) // (2 * experts))
    pairs = expert_ids.reshape(-1)
    onehot = (pairs[:, None] == jnp.arange(experts, dtype=jnp.int32)[None, :]).astype(jnp.int32)
    slot = jnp.sum((jnp.cumsum(onehot, axis=0) - onehot) * onehot, axis=1)
    dest = pairs * capacity + slot
    source_rows = jnp.repeat(tokens, topk, axis=0)
    outgoing = jnp.zeros((experts * capacity, width), jnp.bfloat16).at[dest].set(source_rows)
    outgoing = outgoing.reshape(experts, capacity, width)
    received = lax.all_to_all(outgoing, "block", split_axis=0, concat_axis=0, tiled=True)
    produced = run_expert(received, w_gate[0], w_up[0], w_down[0])
    returned = lax.all_to_all(produced, "block", split_axis=0, concat_axis=0, tiled=True)
    picked = returned.reshape(experts * capacity, width)[dest]
    weighted = picked.astype(jnp.float32).reshape(tok_rows, topk, width) * route_weight[:, :, None]
    return jnp.sum(weighted, axis=1)


def sparse(tokens, expert_ids, route_weight, memory_keep, mem_keys, w_gate, w_up, w_down):
    tok_rows, width = tokens.shape
    moe = sparse_moe(tokens, expert_ids, route_weight, w_gate, w_up, w_down)
    scale_d = width ** (-0.5)
    scores = (jnp.dot(tokens, mem_keys.T, preferred_element_type=jnp.float32) * scale_d).astype(
        jnp.bfloat16
    )
    write = jnp.dot(scores.T, tokens, preferred_element_type=jnp.float32) / tok_rows
    survival_flags = memory_keep[0]
    identity = (jnp.ones_like(survival_flags), jnp.zeros_like(write))
    _, memory_in = prefix((survival_flags, write), "block", chain, identity)
    memory_state = survival_flags[None, :] * memory_in + write
    return finish(tokens, moe, memory_in), memory_state


def finish(tokens, moe, memory_in):
    scale_d = tokens.shape[1] ** (-0.5)
    scale_m = memory_in.shape[0] ** (-0.5)
    memory_read = memory_in.astype(jnp.bfloat16)
    read_scores = (
        jnp.dot(tokens, memory_read.T, preferred_element_type=jnp.float32) * scale_d
    ).astype(jnp.bfloat16)
    recall = jnp.dot(read_scores, memory_read, preferred_element_type=jnp.float32) * scale_m
    return (moe.astype(jnp.float32) + recall).astype(jnp.bfloat16)


def dot(a, b, ca=1, cb=0):
    return lax.dot_general(a, b, (((ca,), (cb,)), ((), ())), preferred_element_type=jnp.float32)


def dense_kernel(
    count,
    tokens_ref,
    ids_ref,
    weight_ref,
    keep_ref,
    keys_ref,
    gate_ref,
    up_ref,
    down_ref,
    mixed_ref,
    state_ref,
    clips,
    aux,
    ids,
    weight,
    keys,
    state,
    mixed,
    gate_w,
    up_w,
    down_w,
    parts,
    taken,
    landed,
    base,
    load_sem,
    out_sem,
    ring_send,
    ring_recv,
    twin_send,
    twin_recv,
    part_send,
    part_recv,
    sum_send,
    sum_recv,
):
    turn = count // 2
    line = turn // 2
    far = turn // 2
    rows, width = tokens_ref.shape
    piece = rows // 2
    part = piece // 2
    hidden_width = gate_w.shape[1]
    mem = keys.shape[0]
    me = lax.axis_index("block")
    core = lax.rem(me, 2)

    def place_of(block):
        x = lax.rem(block // 2, 2)
        z = block // 4
        return x * (2 * line - 1 - z) + (1 - x) * z

    def block_of(place, on):
        x = place // line
        z = x * (2 * line - 1 - place) + (1 - x) * place
        return (z * 2 + x) * 2 + on

    def wrap(value):
        return lax.rem(value + 2 * turn, turn)

    here = place_of(me)
    ahead = block_of(wrap(here + 1), core)
    behind = block_of(wrap(here - 1), core)
    toward = (ahead, behind)
    twin = block_of(here, 1 - core)

    def span(h):
        if isinstance(h, int):
            return pl.ds(h * piece, piece)
        return pl.ds(pl.multiple_of(h * piece, piece), piece)

    def remote(src, dst, send, recv, to):
        return pltpu.make_async_remote_copy(
            src_ref=src,
            dst_ref=dst,
            send_sem=send,
            recv_sem=recv,
            device_id={"block": to},
            device_id_type=pl.DeviceIdType.MESH,
        )

    def hop(d, k, s, place, own=False):
        h = (d + s) % 2 if isinstance(s, int) else lax.rem(d + s, 2)
        dst = clips.at[place, core, span(h)]
        src = tokens_ref.at[span(h)] if own else dst
        return remote(src, dst, ring_send.at[d, s, k], ring_recv.at[d, s, k], toward[d])

    def hop_aux(d, k, place):
        both = aux.at[place, core]
        return remote(both, both, ring_send.at[d, 2, k], ring_recv.at[d, 2, k], toward[d])

    def swap(off, h, on, own=False):
        dst = clips.at[wrap(here + off), on, span(h)]
        src = tokens_ref.at[span(h)] if own else dst
        return remote(src, dst, twin_send.at[h, off], twin_recv.at[h, off], twin)

    def swap_aux(off, on):
        both = aux.at[wrap(here + off), on]
        return remote(both, both, twin_send.at[2, off], twin_recv.at[2, off], twin)

    def pass_part(off, h):
        return remote(
            parts.at[1 - core, off, span(h)],
            taken.at[off, span(h)],
            part_send.at[h, off],
            part_recv.at[h, off],
            twin,
        )

    def pass_sum(d, i, h, q):
        at = pl.ds(h * piece + q * part, part)
        return remote(
            parts.at[core, wrap((1 - 2 * d) * (far - i)), at],
            landed.at[d * far + i, at],
            sum_send.at[d, i, 2 * h + q],
            sum_recv.at[d, i, 2 * h + q],
            toward[d],
        )

    loads = [
        pltpu.make_async_copy(src, dst, load_sem.at[i])
        for i, (src, dst) in enumerate(
            (
                (ids_ref, ids),
                (weight_ref, weight),
                (keep_ref, aux.at[here, core, pl.ds(count, width // rows)]),
                (tokens_ref, clips.at[here, core]),
                (gate_ref.at[0], gate_w),
                (up_ref.at[0], up_w),
                (down_ref.at[0], down_w),
                (keys_ref, keys),
            )
        )
    ]

    barrier = pltpu.get_barrier_semaphore()
    for other in (ahead, behind, twin):
        pl.semaphore_signal(
            barrier, inc=1, device_id={"block": other}, device_id_type=pl.DeviceIdType.MESH
        )
    for load in loads:
        load.start()
    pl.semaphore_wait(barrier, 3)

    for s in range(2):
        for d in range(2):
            hop(d, 1, s, here, True).start()
        swap(0, s, core, True).start()
        if s == 0:
            for load in loads[:3]:
                load.wait()
            for e in range(count):
                named = jnp.where(ids[...] == e, weight[...], 0.0)
                aux[here, core, e : e + 1, :] = jnp.sum(named, axis=0, keepdims=True)
            for d in range(2):
                hop_aux(d, 1, here).start()
            swap_aux(0, core).start()

    scale_d = width ** (-0.5)
    scale_m = mem ** (-0.5)
    down_row = lax.broadcasted_iota(jnp.int32, (piece, rows), 0)
    along = lax.broadcasted_iota(jnp.int32, (piece, rows), 1)

    def column(place, on, h):
        row = jnp.broadcast_to(aux[place, on, pl.ds(me, 1), :], (piece, rows))
        picked = jnp.where(down_row + h * piece == along, row, 0.0)
        return jnp.sum(picked, axis=1, keepdims=True)

    def work(halves):
        pieces = [(off, h, on) for off, h in halves for on in range(2)]
        x = jnp.concatenate([clips[wrap(here + off), on, span(h), :] for off, h, on in pieces], axis=0)
        hidden = []
        for at in range(0, hidden_width, 256):
            cols = slice(at, min(at + 256, hidden_width))
            g = dot(x, gate_w[:, cols])
            u = dot(x, up_w[:, cols])
            hidden.append((g / (1.0 + jnp.exp(-g)) * u).astype(jnp.bfloat16))
        hidden = jnp.concatenate(hidden, axis=1)
        shares = jnp.concatenate([column(wrap(here + off), on, h) for off, h, on in pieces], axis=0)
        for at in range(0, width, 512):
            cols = slice(at, min(at + 512, width))
            out = (dot(hidden, down_w[:, cols]) * shares).astype(jnp.bfloat16)
            for j, (off, h, on) in enumerate(pieces):
                parts[on, off, span(h), cols] = out[j * piece : (j + 1) * piece]
        for off, h in halves:
            pass_part(off, h).start()

    def add_up(off, h, q, addends, place):
        def some(i, _):
            at = pl.ds(pl.multiple_of(h * piece + q * part + i * 16, 16), 16)
            total = parts[core, off, at, :].astype(jnp.float32)
            total = total + taken[off, at, :].astype(jnp.float32)
            for addend in addends:
                total = total + landed[addend, at, :].astype(jnp.float32)
            place(off, at, total)
            return 0

        lax.fori_loop(0, part // 16, some, 0)

    def put(off, at, total):
        parts[core, off, at, :] = total.astype(jnp.bfloat16)

    def pass_on(i, first):
        for d in range(2):
            h = d if first else 1 - d
            off = wrap((1 - 2 * d) * (far - i))
            more = i > (0 if first else 1)
            pass_part(off, h).wait_recv()
            for q in range(2):
                if more:
                    pass_sum(d, i - 1, h, q).wait_recv()
                add_up(off, h, q, [d * far + i - 1] if more else [], put)
                pass_sum(d, i, h, q).start()

    def arrive(d, k, s):
        off = wrap((2 * d - 1) * k)
        place = wrap(here + off)
        h = lax.rem(d + s, 2)
        hop(d, k, s, place).wait_recv()

        @pl.when((k < far - 1) | ((k == far - 1) & (s == 0)))
        def _():
            hop(d, k + 1, s, place).start()

        swap(off, h, core).start()

        @pl.when((s == 0) & (k < far + 1 - d))
        def _():
            hop_aux(d, k, place).wait_recv()

            @pl.when(k < far - d)
            def _():
                hop_aux(d, k + 1, place).start()

            swap_aux(off, core).start()

    def step(t, _):
        k = (t + 1) // 2
        s = lax.rem(t + 1, 2)
        off_a = wrap(-k)
        off_b = wrap(k)

        @pl.when(t == 0)
        def _():
            for load in loads[3:]:
                load.wait()

        @pl.when(t > 0)
        def _():
            arrive(0, k, s)
            arrive(1, k, s)

        @pl.when(t == turn - 2)
        def _():
            pass_on(1, False)

        @pl.when(t == turn - 1)
        def _():
            pass_on(2, False)

        swap(off_a, s, 1 - core).wait_recv()
        swap(off_b, 1 - s, 1 - core).wait_recv()

        @pl.when((s == 0) | (t == 0))
        def _():
            swap_aux(off_a, 1 - core).wait_recv()

        @pl.when((s == 0) & (k < far))
        def _():
            swap_aux(off_b, 1 - core).wait_recv()

        work([(off_a, s), (off_b, 1 - s)])
        return 0

    lax.fori_loop(0, turn, step, 0)
    pass_on(0, True)

    def keep_row(clip):
        block = aux[place_of(clip), lax.rem(clip, 2), count:, :]
        return jnp.concatenate([block[i : i + 1, :] for i in range(block.shape[0])], axis=1)

    def remember(clip):
        x = clips[place_of(clip), lax.rem(clip, 2)]
        scores = (dot(x, keys[...], 1, 1) * scale_d).astype(jnp.bfloat16)
        write = dot(scores, x, 0, 0) * (1.0 / rows)
        state[...] = keep_row(clip) * state[...] + write

    def lap(clip, _):
        @pl.when(clip < me)
        def _():
            remember(clip)

        return 0

    def recall():
        read = state[...].astype(jnp.bfloat16)
        remember(me)
        scores = (dot(clips[here, core], read, 1, 1) * scale_d).astype(jnp.bfloat16)
        for at in range(0, width, 512):
            cols = slice(at, min(at + 512, width))
            base[:, cols] = dot(scores, read[:, cols]) * scale_m

    state[...] = jnp.zeros((mem, width), jnp.float32)
    share = -(-count // (far - 2))
    for i in range(1, far):
        if i < far - 1:
            lax.fori_loop((i - 1) * share, min(i * share, count), lap, 0)
        else:
            recall()
            pltpu.make_async_copy(state, state_ref, out_sem.at[2]).start()
        pass_on(i, True)
        if 2 < i + 2 < far:
            pass_on(i + 2, False)

    def ready(h):
        return pltpu.make_async_copy(mixed.at[span(h)], mixed_ref.at[span(h)], out_sem.at[h])

    def finish_some(off, at, total):
        mixed[at, :] = (total + base[at, :]).astype(jnp.bfloat16)

    for h in range(2):
        pass_part(0, h).wait_recv()
        for q in range(2):
            for d in range(2):
                pass_sum(d, far - 1, h, q).wait_recv()
            add_up(0, h, q, [far - 1, 2 * far - 1], finish_some)
        ready(h).start()

    for d in range(2):
        for k in range(1, far + 1):
            if k < far + 1 - d:
                hop_aux(d, k, here).wait_send()
            for s in range(2 if k < far else 1):
                hop(d, k, s, here).wait_send()
    for off in range(turn):
        swap_aux(off, core).wait_send()
        for h in range(2):
            swap(off, h, core).wait_send()
            pass_part(off, h).wait_send()
    for d in range(2):
        for i in range(far):
            for h in range(2):
                if i > 0 or h == d:
                    for q in range(2):
                        pass_sum(d, i, h, q).wait_send()
    pltpu.make_async_copy(state, state_ref, out_sem.at[2]).wait()
    for h in range(2):
        ready(h).wait()


def settle_kernel(mixed_in, state_in, mixed_ref, state_ref, mixed, state, sem):
    ways = ((mixed_in, mixed, mixed_ref), (state_in, state, state_ref))
    into = [pltpu.make_async_copy(src, mid, sem.at[0, i]) for i, (src, mid, _) in enumerate(ways)]
    out = [pltpu.make_async_copy(mid, dst, sem.at[1, i]) for i, (_, mid, dst) in enumerate(ways)]
    for copy in into:
        copy.start()
    for first, second in zip(into, out):
        first.wait()
        second.start()
    for copy in out:
        copy.wait()


def dense(tokens, expert_ids, route_weight, memory_keep, mem_keys, w_gate, w_up, w_down):
    rows, width = tokens.shape
    topk = expert_ids.shape[1]
    mem = mem_keys.shape[0]
    hidden = w_gate.shape[2]
    count = lax.axis_size("block")
    turn = count // 2
    far = turn // 2
    bf16, f32 = jnp.bfloat16, jnp.float32
    anywhere = pl.BlockSpec(memory_space=pl.ANY)
    dma = pltpu.SemaphoreType.DMA
    shapes = (
        jax.ShapeDtypeStruct((rows, width), bf16),
        jax.ShapeDtypeStruct((mem, width), f32),
    )
    results = pl.pallas_call(
        functools.partial(dense_kernel, count),
        out_shape=shapes,
        in_specs=[anywhere] * 8,
        out_specs=(anywhere, anywhere),
        scratch_shapes=[
            pltpu.VMEM((turn, 2, rows, width), bf16),
            pltpu.VMEM((turn, 2, count + width // rows, rows), f32),
            pltpu.VMEM((topk, rows), jnp.int32),
            pltpu.VMEM((topk, rows), f32),
            pltpu.VMEM((mem, width), bf16),
            pltpu.VMEM((mem, width), f32),
            pltpu.VMEM((rows, width), bf16),
            pltpu.VMEM((width, hidden), bf16),
            pltpu.VMEM((width, hidden), bf16),
            pltpu.VMEM((hidden, width), bf16),
            pltpu.VMEM((2, turn, rows, width), bf16),
            pltpu.VMEM((turn, rows, width), bf16),
            pltpu.VMEM((turn, rows, width), bf16),
            pltpu.VMEM((rows, width), f32),
            dma((8,)),
            dma((3,)),
            dma((2, 3, far + 1)),
            dma((2, 3, far + 1)),
            dma((3, turn)),
            dma((3, turn)),
            dma((2, turn)),
            dma((2, turn)),
            dma((2, far, 4)),
            dma((2, far, 4)),
        ],
        compiler_params=pltpu.CompilerParams(
            collective_id=0, has_side_effects=True, vmem_limit_bytes=56 * 2**20
        ),
        cost_estimate=pl.CostEstimate(
            flops=6 * count * rows * width * hidden, bytes_accessed=2 * 3 * width * hidden, transcendentals=0
        ),
    )(
        tokens,
        expert_ids.T,
        route_weight.T,
        memory_keep.reshape(-1, rows),
        mem_keys,
        w_gate,
        w_up,
        w_down,
    )
    return pl.pallas_call(
        settle_kernel,
        out_shape=shapes,
        in_specs=[anywhere] * 2,
        out_specs=(anywhere, anywhere),
        scratch_shapes=[pltpu.VMEM((rows, width), bf16), pltpu.VMEM((mem, width), f32), dma((2, 2))],
    )(*results)


def solution(mesh):
    experts = mesh.shape["block"]

    def shards(tokens, expert_ids, *rest):
        few = experts <= 4 * expert_ids.shape[1]
        return (dense if few else sparse)(tokens, expert_ids, *rest)

    return jax.shard_map(
        shards,
        mesh=mesh,
        in_specs=(
            P(("groups", "block"), None),
            P(("groups", "block"), None),
            P(("groups", "block"), None),
            P(("groups", "block"), None),
            P(),
            P("block", None, None),
            P("block", None, None),
            P("block", None, None),
        ),
        out_specs=(P(("groups", "block"), None), P(("groups", "block"), None)),
        check_vma=False,
    )
```

```python
import functools

import jax
import jax.numpy as jnp
from jax import lax
from jax.experimental import pallas as pl
from jax.experimental.pallas import tpu as pltpu
from jax.sharding import PartitionSpec as P


def prefix(value, axis, join, neutral):
    count, mine = (lax.axis_size(axis), lax.axis_index(axis))
    pieces = jax.tree.map(lambda part: lax.all_gather(part, axis), value)
    subtotal = jax.tree.map(
        lambda part, zero: jnp.full_like(part, 0) + jnp.asarray(zero, part.dtype), value, neutral
    )

    def lap(position, subtotal):
        longer = join(subtotal, jax.tree.map(lambda part: part[position], pieces))
        return jax.tree.map(lambda new, old: jnp.where(position < mine, new, old), longer, subtotal)

    return lax.fori_loop(0, count - 1, lap, subtotal)


def run_expert(received, gate_w, up_w, down_w):
    count, slots, width = received.shape
    flat = received.reshape(count * slots, width)
    gate = jnp.dot(flat, gate_w, preferred_element_type=jnp.float32)
    upper = jnp.dot(flat, up_w, preferred_element_type=jnp.float32)
    hidden = (jax.nn.silu(gate) * upper).astype(jnp.bfloat16)
    produced = jnp.dot(hidden, down_w, preferred_element_type=jnp.float32).astype(jnp.bfloat16)
    return produced.reshape(count, slots, width)


def chain(earlier, later):
    return (earlier[0] * later[0], later[0][None, :] * earlier[1] + later[1])


def sparse_moe(tokens, expert_ids, route_weight, w_gate, w_up, w_down):
    tok_rows, width = tokens.shape
    topk = expert_ids.shape[1]
    experts = lax.axis_size("block")
    capacity = max(2, (3 * tok_rows * topk + 2 * experts - 1) // (2 * experts))
    pairs = expert_ids.reshape(-1)
    onehot = (pairs[:, None] == jnp.arange(experts, dtype=jnp.int32)[None, :]).astype(jnp.int32)
    slot = jnp.sum((jnp.cumsum(onehot, axis=0) - onehot) * onehot, axis=1)
    dest = pairs * capacity + slot
    source_rows = jnp.repeat(tokens, topk, axis=0)
    outgoing = jnp.zeros((experts * capacity, width), jnp.bfloat16).at[dest].set(source_rows)
    outgoing = outgoing.reshape(experts, capacity, width)
    received = lax.all_to_all(outgoing, "block", split_axis=0, concat_axis=0, tiled=True)
    produced = run_expert(received, w_gate[0], w_up[0], w_down[0])
    returned = lax.all_to_all(produced, "block", split_axis=0, concat_axis=0, tiled=True)
    picked = returned.reshape(experts * capacity, width)[dest]
    weighted = picked.astype(jnp.float32).reshape(tok_rows, topk, width) * route_weight[:, :, None]
    return jnp.sum(weighted, axis=1)


def sparse(tokens, expert_ids, route_weight, memory_keep, mem_keys, w_gate, w_up, w_down):
    tok_rows, width = tokens.shape
    moe = sparse_moe(tokens, expert_ids, route_weight, w_gate, w_up, w_down)
    scale_d = width ** (-0.5)
    scores = (jnp.dot(tokens, mem_keys.T, preferred_element_type=jnp.float32) * scale_d).astype(
        jnp.bfloat16
    )
    write = jnp.dot(scores.T, tokens, preferred_element_type=jnp.float32) / tok_rows
    survival_flags = memory_keep[0]
    identity = (jnp.ones_like(survival_flags), jnp.zeros_like(write))
    _, memory_in = prefix((survival_flags, write), "block", chain, identity)
    memory_state = survival_flags[None, :] * memory_in + write
    return finish(tokens, moe, memory_in), memory_state


def finish(tokens, moe, memory_in):
    scale_d = tokens.shape[1] ** (-0.5)
    scale_m = memory_in.shape[0] ** (-0.5)
    memory_read = memory_in.astype(jnp.bfloat16)
    read_scores = (
        jnp.dot(tokens, memory_read.T, preferred_element_type=jnp.float32) * scale_d
    ).astype(jnp.bfloat16)
    recall = jnp.dot(read_scores, memory_read, preferred_element_type=jnp.float32) * scale_m
    return (moe.astype(jnp.float32) + recall).astype(jnp.bfloat16)


def dot(a, b, ca=1, cb=0):
    return lax.dot_general(a, b, (((ca,), (cb,)), ((), ())), preferred_element_type=jnp.float32)


def dense_kernel(
    count,
    tokens_ref,
    ids_ref,
    weight_ref,
    keep_ref,
    keys_ref,
    gate_ref,
    up_ref,
    down_ref,
    mixed_ref,
    state_ref,
    clips,
    aux,
    ids,
    weight,
    keys,
    state,
    mixed,
    gate_w,
    up_w,
    down_w,
    parts,
    taken,
    landed,
    base,
    load_sem,
    out_sem,
    ring_send,
    ring_recv,
    twin_send,
    twin_recv,
    part_send,
    part_recv,
    sum_send,
    sum_recv,
):
    cuts = 4
    turn = count // 2
    line = turn // 2
    far = turn // 2
    rows, width = tokens_ref.shape
    piece = rows // 2
    part = piece // cuts
    hidden_width = gate_w.shape[1]
    mem = keys.shape[0]
    me = lax.axis_index("block")
    core = lax.rem(me, 2)

    def place_of(block):
        x = lax.rem(block // 2, 2)
        z = block // 4
        return x * (2 * line - 1 - z) + (1 - x) * z

    def block_of(place, on):
        x = place // line
        z = x * (2 * line - 1 - place) + (1 - x) * place
        return (z * 2 + x) * 2 + on

    def wrap(value):
        return lax.rem(value + 2 * turn, turn)

    here = place_of(me)
    ahead = block_of(wrap(here + 1), core)
    behind = block_of(wrap(here - 1), core)
    toward = (ahead, behind)
    twin = block_of(here, 1 - core)

    def span(h):
        if isinstance(h, int):
            return pl.ds(h * piece, piece)
        return pl.ds(pl.multiple_of(h * piece, piece), piece)

    def remote(src, dst, send, recv, to):
        return pltpu.make_async_remote_copy(
            src_ref=src,
            dst_ref=dst,
            send_sem=send,
            recv_sem=recv,
            device_id={"block": to},
            device_id_type=pl.DeviceIdType.MESH,
        )

    def hop(d, k, s, place, own=False):
        h = (d + s) % 2 if isinstance(s, int) else lax.rem(d + s, 2)
        dst = clips.at[place, core, span(h)]
        src = tokens_ref.at[span(h)] if own else dst
        return remote(src, dst, ring_send.at[d, s, k], ring_recv.at[d, s, k], toward[d])

    def hop_aux(d, k, place):
        both = aux.at[place, core]
        return remote(both, both, ring_send.at[d, 2, k], ring_recv.at[d, 2, k], toward[d])

    def swap(off, h, on, own=False):
        dst = clips.at[wrap(here + off), on, span(h)]
        src = tokens_ref.at[span(h)] if own else dst
        return remote(src, dst, twin_send.at[h, off], twin_recv.at[h, off], twin)

    def swap_aux(off, on):
        both = aux.at[wrap(here + off), on]
        return remote(both, both, twin_send.at[2, off], twin_recv.at[2, off], twin)

    def pass_part(off, h):
        return remote(
            parts.at[1 - core, off, span(h)],
            taken.at[off, span(h)],
            part_send.at[h, off],
            part_recv.at[h, off],
            twin,
        )

    def pass_sum(d, i, h, q):
        at = pl.ds(h * piece + q * part, part)
        return remote(
            parts.at[core, wrap((1 - 2 * d) * (far - i)), at],
            landed.at[d * far + i, at],
            sum_send.at[d, i, cuts * h + q],
            sum_recv.at[d, i, cuts * h + q],
            toward[d],
        )

    loads = [
        pltpu.make_async_copy(src, dst, load_sem.at[i])
        for i, (src, dst) in enumerate(
            (
                (ids_ref, ids),
                (weight_ref, weight),
                (keep_ref, aux.at[here, core, pl.ds(count, width // rows)]),
                (tokens_ref, clips.at[here, core]),
                (gate_ref.at[0], gate_w),
                (up_ref.at[0], up_w),
                (down_ref.at[0], down_w),
                (keys_ref, keys),
            )
        )
    ]

    barrier = pltpu.get_barrier_semaphore()
    for other in (ahead, behind, twin):
        pl.semaphore_signal(
            barrier, inc=1, device_id={"block": other}, device_id_type=pl.DeviceIdType.MESH
        )
    for load in loads:
        load.start()
    pl.semaphore_wait(barrier, 3)

    for s in range(2):
        for d in range(2):
            hop(d, 1, s, here, True).start()
        swap(0, s, core, True).start()
        if s == 0:
            for load in loads[:3]:
                load.wait()
            for e in range(count):
                named = jnp.where(ids[...] == e, weight[...], 0.0)
                aux[here, core, e : e + 1, :] = jnp.sum(named, axis=0, keepdims=True)
            for d in range(2):
                hop_aux(d, 1, here).start()
            swap_aux(0, core).start()

    scale_d = width ** (-0.5)
    scale_m = mem ** (-0.5)
    down_row = lax.broadcasted_iota(jnp.int32, (piece, rows), 0)
    along = lax.broadcasted_iota(jnp.int32, (piece, rows), 1)

    def column(place, on, h):
        row = jnp.broadcast_to(aux[place, on, pl.ds(me, 1), :], (piece, rows))
        picked = jnp.where(down_row + h * piece == along, row, 0.0)
        return jnp.sum(picked, axis=1, keepdims=True)

    def work(halves):
        pieces = [(off, h, on) for off, h in halves for on in range(2)]
        x = jnp.concatenate([clips[wrap(here + off), on, span(h), :] for off, h, on in pieces], axis=0)
        hidden = []
        for at in range(0, hidden_width, 256):
            cols = slice(at, min(at + 256, hidden_width))
            g = dot(x, gate_w[:, cols])
            u = dot(x, up_w[:, cols])
            hidden.append((g / (1.0 + jnp.exp(-g)) * u).astype(jnp.bfloat16))
        hidden = jnp.concatenate(hidden, axis=1)
        shares = jnp.concatenate([column(wrap(here + off), on, h) for off, h, on in pieces], axis=0)
        for at in range(0, width, 512):
            cols = slice(at, min(at + 512, width))
            out = (dot(hidden, down_w[:, cols]) * shares).astype(jnp.bfloat16)
            for j, (off, h, on) in enumerate(pieces):
                parts[on, off, span(h), cols] = out[j * piece : (j + 1) * piece]
        for off, h in halves:
            pass_part(off, h).start()

    def add_up(off, h, q, addends, place):
        def some(i, _):
            at = pl.ds(pl.multiple_of(h * piece + q * part + i * 16, 16), 16)
            total = parts[core, off, at, :].astype(jnp.float32)
            total = total + taken[off, at, :].astype(jnp.float32)
            for addend in addends:
                total = total + landed[addend, at, :].astype(jnp.float32)
            place(off, at, total)
            return 0

        lax.fori_loop(0, part // 16, some, 0)

    def put(off, at, total):
        parts[core, off, at, :] = total.astype(jnp.bfloat16)

    def pass_on(i, first):
        for d in range(2):
            h = d if first else 1 - d
            off = wrap((1 - 2 * d) * (far - i))
            more = i > (0 if first else 1)
            pass_part(off, h).wait_recv()
            for q in range(cuts):
                if more:
                    pass_sum(d, i - 1, h, q).wait_recv()
                add_up(off, h, q, [d * far + i - 1] if more else [], put)
                pass_sum(d, i, h, q).start()

    def arrive(d, k, s):
        off = wrap((2 * d - 1) * k)
        place = wrap(here + off)
        h = lax.rem(d + s, 2)
        hop(d, k, s, place).wait_recv()

        @pl.when((k < far - 1) | ((k == far - 1) & (s == 0)))
        def _():
            hop(d, k + 1, s, place).start()

        swap(off, h, core).start()

        @pl.when((s == 0) & (k < far + 1 - d))
        def _():
            hop_aux(d, k, place).wait_recv()

            @pl.when(k < far - d)
            def _():
                hop_aux(d, k + 1, place).start()

            swap_aux(off, core).start()

    def step(t, _):
        k = (t + 1) // 2
        s = lax.rem(t + 1, 2)
        off_a = wrap(-k)
        off_b = wrap(k)

        @pl.when(t == 0)
        def _():
            for load in loads[3:]:
                load.wait()

        @pl.when(t == turn - 2)
        def _():
            pass_on(1, False)

        @pl.when(t > 0)
        def _():
            arrive(0, k, s)
            arrive(1, k, s)

        @pl.when(t == turn - 1)
        def _():
            pass_on(2, False)

        swap(off_a, s, 1 - core).wait_recv()
        swap(off_b, 1 - s, 1 - core).wait_recv()

        @pl.when((s == 0) | (t == 0))
        def _():
            swap_aux(off_a, 1 - core).wait_recv()

        @pl.when((s == 0) & (k < far))
        def _():
            swap_aux(off_b, 1 - core).wait_recv()

        work([(off_a, s), (off_b, 1 - s)])
        return 0

    lax.fori_loop(0, turn, step, 0)
    pass_on(0, True)

    def keep_row(clip):
        block = aux[place_of(clip), lax.rem(clip, 2), count:, :]
        return jnp.concatenate([block[i : i + 1, :] for i in range(block.shape[0])], axis=1)

    def remember(clip):
        x = clips[place_of(clip), lax.rem(clip, 2)]
        scores = (dot(x, keys[...], 1, 1) * scale_d).astype(jnp.bfloat16)
        write = dot(scores, x, 0, 0) * (1.0 / rows)
        state[...] = keep_row(clip) * state[...] + write

    def lap(clip, _):
        @pl.when(clip < me)
        def _():
            remember(clip)

        return 0

    def recall():
        read = state[...].astype(jnp.bfloat16)
        remember(me)
        scores = (dot(clips[here, core], read, 1, 1) * scale_d).astype(jnp.bfloat16)
        for at in range(0, width, 512):
            cols = slice(at, min(at + 512, width))
            base[:, cols] = dot(scores, read[:, cols]) * scale_m

    state[...] = jnp.zeros((mem, width), jnp.float32)
    share = -(-count // (far - 2))
    for i in range(1, far):
        if i < far - 1:
            lax.fori_loop((i - 1) * share, min(i * share, count), lap, 0)
        else:
            recall()
            pltpu.make_async_copy(state, state_ref, out_sem.at[2]).start()
        pass_on(i, True)
        if 2 < i + 2 < far:
            pass_on(i + 2, False)

    def ready(h):
        return pltpu.make_async_copy(mixed.at[span(h)], mixed_ref.at[span(h)], out_sem.at[h])

    def finish_some(off, at, total):
        mixed[at, :] = (total + base[at, :]).astype(jnp.bfloat16)

    for h in range(2):
        pass_part(0, h).wait_recv()
        for q in range(cuts):
            for d in range(2):
                pass_sum(d, far - 1, h, q).wait_recv()
            add_up(0, h, q, [far - 1, 2 * far - 1], finish_some)
        ready(h).start()

    for d in range(2):
        for k in range(1, far + 1):
            if k < far + 1 - d:
                hop_aux(d, k, here).wait_send()
            for s in range(2 if k < far else 1):
                hop(d, k, s, here).wait_send()
    for off in range(turn):
        swap_aux(off, core).wait_send()
        for h in range(2):
            swap(off, h, core).wait_send()
            pass_part(off, h).wait_send()
    for d in range(2):
        for i in range(far):
            for h in range(2):
                if i > 0 or h == d:
                    for q in range(cuts):
                        pass_sum(d, i, h, q).wait_send()
    pltpu.make_async_copy(state, state_ref, out_sem.at[2]).wait()
    for h in range(2):
        ready(h).wait()


def settle_kernel(mixed_in, state_in, mixed_ref, state_ref, mixed, state, sem):
    ways = ((mixed_in, mixed, mixed_ref), (state_in, state, state_ref))
    into = [pltpu.make_async_copy(src, mid, sem.at[0, i]) for i, (src, mid, _) in enumerate(ways)]
    out = [pltpu.make_async_copy(mid, dst, sem.at[1, i]) for i, (_, mid, dst) in enumerate(ways)]
    for copy in into:
        copy.start()
    for first, second in zip(into, out):
        first.wait()
        second.start()
    for copy in out:
        copy.wait()


def dense(tokens, expert_ids, route_weight, memory_keep, mem_keys, w_gate, w_up, w_down):
    rows, width = tokens.shape
    topk = expert_ids.shape[1]
    mem = mem_keys.shape[0]
    hidden = w_gate.shape[2]
    count = lax.axis_size("block")
    turn = count // 2
    far = turn // 2
    bf16, f32 = jnp.bfloat16, jnp.float32
    anywhere = pl.BlockSpec(memory_space=pl.ANY)
    dma = pltpu.SemaphoreType.DMA
    shapes = (
        jax.ShapeDtypeStruct((rows, width), bf16),
        jax.ShapeDtypeStruct((mem, width), f32),
    )
    results = pl.pallas_call(
        functools.partial(dense_kernel, count),
        out_shape=shapes,
        in_specs=[anywhere] * 8,
        out_specs=(anywhere, anywhere),
        scratch_shapes=[
            pltpu.VMEM((turn, 2, rows, width), bf16),
            pltpu.VMEM((turn, 2, count + width // rows, rows), f32),
            pltpu.VMEM((topk, rows), jnp.int32),
            pltpu.VMEM((topk, rows), f32),
            pltpu.VMEM((mem, width), bf16),
            pltpu.VMEM((mem, width), f32),
            pltpu.VMEM((rows, width), bf16),
            pltpu.VMEM((width, hidden), bf16),
            pltpu.VMEM((width, hidden), bf16),
            pltpu.VMEM((hidden, width), bf16),
            pltpu.VMEM((2, turn, rows, width), bf16),
            pltpu.VMEM((turn, rows, width), bf16),
            pltpu.VMEM((turn, rows, width), bf16),
            pltpu.VMEM((rows, width), f32),
            dma((8,)),
            dma((3,)),
            dma((2, 3, far + 1)),
            dma((2, 3, far + 1)),
            dma((3, turn)),
            dma((3, turn)),
            dma((2, turn)),
            dma((2, turn)),
            dma((2, far, 8)),
            dma((2, far, 8)),
        ],
        compiler_params=pltpu.CompilerParams(
            collective_id=0, has_side_effects=True, vmem_limit_bytes=56 * 2**20
        ),
        cost_estimate=pl.CostEstimate(
            flops=6 * count * rows * width * hidden, bytes_accessed=2 * 3 * width * hidden, transcendentals=0
        ),
    )(
        tokens,
        expert_ids.T,
        route_weight.T,
        memory_keep.reshape(-1, rows),
        mem_keys,
        w_gate,
        w_up,
        w_down,
    )
    return pl.pallas_call(
        settle_kernel,
        out_shape=shapes,
        in_specs=[anywhere] * 2,
        out_specs=(anywhere, anywhere),
        scratch_shapes=[pltpu.VMEM((rows, width), bf16), pltpu.VMEM((mem, width), f32), dma((2, 2))],
    )(*results)


def solution(mesh):
    experts = mesh.shape["block"]

    def shards(tokens, expert_ids, *rest):
        few = experts <= 4 * expert_ids.shape[1]
        return (dense if few else sparse)(tokens, expert_ids, *rest)

    return jax.shard_map(
        shards,
        mesh=mesh,
        in_specs=(
            P(("groups", "block"), None),
            P(("groups", "block"), None),
            P(("groups", "block"), None),
            P(("groups", "block"), None),
            P(),
            P("block", None, None),
            P("block", None, None),
            P("block", None, None),
        ),
        out_specs=(P(("groups", "block"), None), P(("groups", "block"), None)),
        check_vma=False,
    )
```
